32 devices in a mesh: row: 8 (over y, x, core), col: 4 (over z).
Axes of the slice: x: 2, y: 2, z: 4, core: 2. Of those that a mesh axis runs over, the one named last changes fastest.
Arguments:
- feats: bfloat16 [1024, 8192], P('col', 'row'), may hold values from -6 to 6
- w_self: bfloat16 [1024, 1024], P('col'), may hold values from -0.1875 to 0.1875
- w_neigh: bfloat16 [1024, 1024], P('col'), may hold values from -0.375 to 0.375
- cotangent: bfloat16 [1024, 8192], P('col', 'row'), may hold values from -6 to 6
- loc_nbr: int32 [8192, 8], P('row'), may hold values from 0 to 1023
- send_rows: int32 [8, 8, 128], P('row'), may hold values from 0 to 1023
- recv_node: int32 [8, 8, 128], P('row'), may hold values from -1 to 1023, as said below
- hub_rows: int32 [128], P('row'), may hold values from 0 to 1023
- hub_nbr: int32 [8192, 2], P('row'), may hold values from 0 to 127
Outputs:
- hidden_out: bfloat16 [1024, 8192], P('col', 'row')
- grad_feats: bfloat16 [1024, 8192], P('col', 'row')
- grad_self: float32 [1024, 1024], P('col')
- grad_neigh: float32 [1024, 1024], P('col')
The draws below stay inside these ranges and needn't reach their ends.
Inputs may be any that keep to these rules, and one draw needn't show every extreme that they name: `recv_node`: for receiver block d and sender block s, the first c slots hold rows of block d and the rest hold -1, with 1 <= c <= 128; in every draw one receiver block gets all 128 slots from every sender block.
All inputs are finite; a program needn't handle non-finite values.
Results may differ from the reference program's by a relative error of at most 0.0075.
Values may be sent and summed in bfloat16 or wider, within the bound.
A program may use at most 64 MiB of HBM per device.

```python
import math
import jax
import jax.numpy as jnp
import numpy as np

F = 1024
NODE_DEV = 1024
SEND = 128
HUB_DEV = 16
K_LOC = 8
K_HUB = 2
NODES = 8192
HUBS = 128
N_ROW = 8


def draw_recv_node(key, part):
    key = jax.random.fold_in(key, 11)
    key_first, key_second, key_hot, key_node = jax.random.split(key, 4)
    first = jax.random.randint(key_first, (N_ROW, N_ROW), 0, SEND + 1)
    second = jax.random.randint(key_second, (N_ROW, N_ROW), 0, SEND + 1)
    counts = 1 + first * second // (SEND + 1)
    hot_block = jax.random.randint(key_hot, (), 0, N_ROW)
    receiver = jnp.arange(N_ROW)[:, None] + jnp.zeros((N_ROW, N_ROW), jnp.int32)
    counts = jnp.where(receiver == hot_block, SEND, counts)
    chosen = jax.random.randint(key_node, (N_ROW, N_ROW, SEND), 0, NODE_DEV)
    position = jnp.arange(SEND)[None, None, :]
    return jnp.where(position < counts[:, :, None], chosen, -1).astype(jnp.int32)


def plant(values, stream_key, smallest, largest):
    spot = [jax.random.randint(jax.random.fold_in(stream_key, axis), (), 0, length) for axis, length in enumerate(values.shape)]
    longest = values.shape.index(max(values.shape))
    beside = spot[:longest] + [(spot[longest] + 1) % values.shape[longest]] + spot[longest + 1:]
    return values.at[tuple(spot)].set(smallest).at[tuple(beside)].set(largest)


def steps_of(key, extent, cuts, smallest, top_value):
    factor_of = 1.0
    for dim, parts in cuts:
        steps = jax.random.uniform(jax.random.fold_in(jax.random.fold_in(key, 6), dim), (parts,), jnp.float32, smallest / len(cuts), top_value / len(cuts))
        factor_of = factor_of * jnp.repeat(jnp.exp(steps), extent[dim] // parts).reshape((-1,) + (1,) * (len(extent) - 1 - dim))
    return factor_of


def rank_table(number_of, lean):
    portions = [(1 << 20) // math.isqrt(standing ** lean) + 1 for standing in range(1, number_of + 1)]
    scale = 1 + sum(portions) // (1 << 30)
    return np.cumsum(np.array([max(1, weight // scale) for weight in portions]))


def ranked(stream_key, shape, amount, lean):
    table = rank_table(amount, lean)
    pick = jax.random.randint(jax.random.fold_in(stream_key, 1), shape, 0, int(table[amount - 1]))
    grade = jnp.searchsorted(jnp.asarray(table, jnp.int32), pick, side="right")
    return jax.random.permutation(jax.random.fold_in(stream_key, 2), amount)[grade].astype(jnp.int32)


def scatter_about(own_key, extent, width, bound, shards=(), held_as=jnp.bfloat16):
    entries = jax.random.normal(own_key, extent, jnp.float32) * width
    if len(shards) > 0:
        entries = steps_of(own_key, extent, shards, -0.22, 0.18) * entries
    return jnp.clip(entries, min=-bound, max=bound).astype(held_as)


def setup_inputs(seed: int = 0) -> dict:
    splits = jax.random.split(jax.random.key(seed), 10)
    return {
        "feats": scatter_about(splits[0], (F, NODES), 1.0, 6.0, ((0, 4), (1, 8))),
        "w_self": scatter_about(splits[1], (F, F), F ** -0.5, 0.1875, ((0, 4),)),
        "w_neigh": scatter_about(splits[2], (F, F), (F // 4) ** -0.5, 0.375, ((0, 4),)),
        "cotangent": scatter_about(splits[3], (F, NODES), 1.0, 6.0, ((0, 4), (1, 8))),
        "loc_nbr": plant(jax.random.randint(splits[4], (NODES, K_LOC), 0, NODE_DEV), jax.random.fold_in(splits[4], 1), 0, NODE_DEV - 1).astype(jnp.int32),
        "send_rows": plant(jax.random.randint(splits[5], (N_ROW, N_ROW, SEND), 0, NODE_DEV), jax.random.fold_in(splits[5], 1), 0, NODE_DEV - 1).astype(jnp.int32),
        "recv_node": draw_recv_node(jax.random.fold_in(splits[9], 71), 0),
        "hub_rows": plant(jax.random.randint(splits[7], (HUBS,), 0, NODE_DEV), jax.random.fold_in(splits[7], 1), 0, NODE_DEV - 1).astype(jnp.int32),
        "hub_nbr": plant(ranked(splits[8], (NODES, K_HUB), HUBS, 2), jax.random.fold_in(splits[8], 3), 0, HUBS - 1).astype(jnp.int32),
    }


def silu_slope(preact):
    sigmoid_part = jax.nn.sigmoid(preact)
    return sigmoid_part * (1.0 + preact * (1.0 - sigmoid_part))


def reference(feats, w_self, w_neigh, cotangent, loc_nbr, send_rows, recv_node, hub_rows, hub_nbr):
    node_rows = feats.T
    node_slopes = cotangent.T
    node_total = node_rows.shape[0]
    block_base = (jnp.arange(node_total, dtype=jnp.int32) // NODE_DEV) * NODE_DEV
    local_global = loc_nbr + block_base[:, None]
    hub_nodes = (jnp.arange(HUBS, dtype=jnp.int32) // HUB_DEV) * NODE_DEV + hub_rows
    hub_global = hub_nodes[hub_nbr]
    owners = jnp.arange(N_ROW, dtype=jnp.int32)
    source = (owners[:, None, None] * NODE_DEV + send_rows).reshape(-1)
    arriving = jnp.transpose(recv_node, (1, 0, 2))
    live_slots = arriving >= 0
    target = jnp.where(live_slots, owners[None, :, None] * NODE_DEV + arriving, node_total).reshape(-1)
    live_flat = live_slots.reshape(-1).astype(jnp.float32)

    local_sum = jnp.zeros(node_rows.shape, jnp.float32)
    for neighbour in range(K_LOC):
        local_sum = local_sum + node_rows[local_global[:, neighbour]].astype(jnp.float32)
    hub_sum = jnp.zeros(node_rows.shape, jnp.float32)
    for neighbour in range(K_HUB):
        hub_sum = hub_sum + node_rows[hub_global[:, neighbour]].astype(jnp.float32)
    remote_sum = jax.ops.segment_sum(node_rows[source].astype(jnp.float32), target, node_total + 1)[:node_total]
    arrivals = jax.ops.segment_sum(live_flat, target, node_total + 1)[:node_total]
    degree = (K_LOC + K_HUB) + arrivals
    agg = ((local_sum + hub_sum + remote_sum) / degree[:, None]).astype(jnp.bfloat16)

    preact = jnp.dot(node_rows, w_self, preferred_element_type=jnp.float32)
    preact = preact + jnp.dot(agg, w_neigh, preferred_element_type=jnp.float32)
    hidden_out = jax.nn.silu(preact).astype(jnp.bfloat16)

    slopes = (node_slopes.astype(jnp.float32) * silu_slope(preact)).astype(jnp.bfloat16)
    grad_self = jnp.dot(node_rows.T, slopes, preferred_element_type=jnp.float32)
    grad_neigh = jnp.dot(agg.T, slopes, preferred_element_type=jnp.float32)
    direct = jnp.dot(slopes, w_self.T, preferred_element_type=jnp.float32)
    back_agg = jnp.dot(slopes, w_neigh.T, preferred_element_type=jnp.float32)
    share_back = (back_agg / degree[:, None]).astype(jnp.bfloat16)
    share_wide = share_back.astype(jnp.float32)

    gathered_back = jnp.zeros(node_rows.shape, jnp.float32)
    for neighbour in range(K_LOC):
        gathered_back = gathered_back + jax.ops.segment_sum(share_wide, local_global[:, neighbour], node_total)
    for neighbour in range(K_HUB):
        gathered_back = gathered_back + jax.ops.segment_sum(share_wide, hub_global[:, neighbour], node_total)
    share_padded = jnp.concatenate([share_wide, jnp.zeros((1, share_wide.shape[1]), jnp.float32)], axis=0)
    gathered_back = gathered_back + jax.ops.segment_sum(share_padded[target], source, node_total)
    grad_feats = (direct + gathered_back).astype(jnp.bfloat16)
    return (hidden_out.T, grad_feats.T, grad_self, grad_neigh)
```

```python
import jax
import jax.numpy as jnp
from jax import lax
from jax.sharding import PartitionSpec as P

BF16 = jnp.bfloat16
F32 = jnp.float32


def silu_slope(preact):
    sigmoid_part = jax.nn.sigmoid(preact)
    return sigmoid_part * (1.0 + preact * (1.0 - sigmoid_part))


def dot(a, b, ca, cb):
    return lax.dot_general(a, b, (((ca,), (cb,)), ((), ())), preferred_element_type=F32)


def picks(indices, size):
    rows = lax.broadcasted_iota(jnp.int32, (size, indices.shape[1]), 0)
    total = (rows == indices[0:1]).astype(F32)
    for k in range(1, indices.shape[0]):
        total = total + (rows == indices[k : k + 1]).astype(F32)
    return total.astype(BF16)


def per_device(feats, w_self, w_neigh, cotangent, loc_nbr, send_rows, recv_node, hub_rows, hub_nbr):
    narrow, nodes = feats.shape
    peers = lax.axis_size("row")
    send_pick = picks(send_rows.reshape(1, -1), nodes)
    recv_pick = picks(recv_node.reshape(1, -1), nodes)
    loc_pick = picks(loc_nbr.T, nodes)
    hub_pick = picks(hub_nbr.T, peers * hub_rows.shape[0])
    own_pick = picks(hub_rows.reshape(1, -1), nodes)

    outgoing = dot(feats, send_pick, 1, 0).astype(BF16).reshape(narrow, peers, -1)
    incoming = lax.all_to_all(outgoing, "row", split_axis=1, concat_axis=1, tiled=True)
    hub_table = lax.all_gather(dot(own_pick, feats, 0, 1).astype(BF16), "row", axis=0, tiled=True)
    arrivals = jnp.sum((recv_pick).astype(F32), axis=1)
    degree = (loc_nbr.shape[1] + hub_nbr.shape[1] + arrivals)[None, :]
    total = dot(feats, loc_pick, 1, 0) + dot(hub_table, hub_pick, 0, 0)
    total = total + dot(incoming.reshape(narrow, -1), recv_pick, 1, 1)
    agg = (total / degree).astype(BF16)
    joined = jnp.concatenate([feats, agg], axis=0)
    weights = jnp.concatenate([w_self, w_neigh], axis=0)
    partial = dot(weights, joined, 0, 0).astype(BF16)
    preact = lax.psum_scatter(partial, "col", scatter_dimension=0, tiled=True).astype(F32)
    hidden_out = jax.nn.silu(preact).astype(BF16)
    slopes = (cotangent.astype(F32) * silu_slope(preact)).astype(BF16)
    wide = lax.all_gather(slopes, "col", axis=0, tiled=True)
    back = dot(weights, wide, 1, 0)
    share = (back[narrow:] / degree).astype(BF16)
    weight_total = lax.psum(dot(joined, wide, 1, 1), "row")
    hub_part = dot(hub_pick, share, 1, 1)
    owned = lax.psum_scatter(hub_part, "row", scatter_dimension=0, tiled=True)
    high = owned.astype(BF16)
    low = (owned - high.astype(F32)).astype(BF16)
    slot_values = dot(share, recv_pick, 1, 0).astype(BF16).reshape(narrow, peers, -1)
    returned = lax.all_to_all(slot_values, "row", split_axis=1, concat_axis=1, tiled=True)
    grad = back[:narrow] + dot(share, loc_pick, 1, 1)
    grad = grad + dot(high, own_pick, 0, 1) + dot(low, own_pick, 0, 1)
    grad = grad + dot(returned.reshape(narrow, -1), send_pick, 1, 1)
    return hidden_out, grad.astype(BF16), weight_total[:narrow], weight_total[narrow:]


def solution(mesh):
    return jax.shard_map(
        per_device,
        mesh=mesh,
        in_specs=(
            P("col", "row"),
            P("col", None),
            P("col", None),
            P("col", "row"),
            P("row", None),
            P("row", None, None),
            P("row", None, None),
            P("row"),
            P("row", None),
        ),
        out_specs=(P("col", "row"), P("col", "row"), P("col", None), P("col", None)),
        check_vma=False,
    )
```

```python
import functools

import jax
import jax.numpy as jnp
from jax import lax
from jax.experimental import pallas as pl
from jax.experimental.pallas import tpu as pltpu
from jax.sharding import PartitionSpec as P

BF16 = jnp.bfloat16
F32 = jnp.float32
MESH = pl.DeviceIdType.MESH


def dot(a, b, ca, cb):
    return lax.dot_general(a, b, (((ca,), (cb,)), ((), ())), preferred_element_type=F32)


def fill_picks(dest, indices, strip):
    size = dest.shape[0]
    strip = min(strip, size)

    def body(i, carry):
        first = pl.multiple_of(i * strip, strip)
        rows = lax.broadcasted_iota(jnp.int32, (strip, indices.shape[1]), 0) + first
        total = jnp.where(rows == indices[0:1, :], 1.0, 0.0)
        for k in range(1, indices.shape[0]):
            total = total + jnp.where(rows == indices[k : k + 1, :], 1.0, 0.0)
        dest[pl.ds(first, strip), :] = total.astype(BF16)
        return carry

    lax.fori_loop(0, size // strip, body, 0)


def layer_kernel(
    n, peers, chunks,
    feats, w_self, w_neigh, w_turned, cot, loc, send, recv, hub_col, hub,
    hidden, grad_feats, grad_self, grad_neigh,
    loc_pick, send_pick, recv_pick, hub_pick, own_pick, degree,
    slot_out, slot_in, hub_out, hub_in,
    total, joined, from_left, from_right, to_left, to_right, slopes,
    direct, share, weight_acc, weight_out, weight_in, weight_sum, weight_all,
    back_out, back_in, hub_back_out, hub_back_in,
    row_send, row_recv, sum_send, sum_recv, spread_send, spread_recv,
):
    narrow, nodes = feats.shape
    width = nodes // chunks
    slots = send.shape[1] // peers
    hubs = hub_col.shape[0]
    me = lax.axis_index("row")
    pos = lax.axis_index("col")
    has_left = pos > 0
    has_right = pos < n - 1

    def row_peer(d):
        return lax.rem(me + d, peers)

    def row_source(d):
        return lax.rem(me + peers - d, peers)

    barrier = pltpu.get_barrier_semaphore()
    for d in range(1, peers):
        pl.semaphore_signal(barrier, inc=1, device_id={"row": row_peer(d)}, device_id_type=MESH)

    @pl.when(has_left)
    def _():
        pl.semaphore_signal(barrier, inc=1, device_id={"col": pos - 1}, device_id_type=MESH)

    @pl.when(has_right)
    def _():
        pl.semaphore_signal(barrier, inc=1, device_id={"col": pos + 1}, device_id_type=MESH)

    def cols(index, size):
        return pl.ds(pl.multiple_of(index * size, size), size)

    def row_copy(src, dst, kind, d):
        return pltpu.make_async_remote_copy(
            src_ref=src, dst_ref=dst, send_sem=row_send.at[kind, d], recv_sem=row_recv.at[kind, d],
            device_id={"row": row_peer(d)}, device_id_type=MESH,
        )

    def slot_copy(d):
        return row_copy(slot_out.at[:, cols(row_peer(d), slots)], slot_in.at[:, cols(me, slots)], 0, d)

    def hub_copy(d):
        return row_copy(hub_out, hub_in.at[cols(me, hubs), :], 1, d)

    def back_copy(d):
        return row_copy(back_out.at[:, cols(row_peer(d), slots)], back_in.at[:, cols(me, slots)], 2, d)

    def hub_back_copy(d):
        return row_copy(hub_back_out.at[cols(row_peer(d), hubs), :], hub_back_in.at[me], 3, d)

    lane_parts = min(peers, weight_acc.shape[1] // 128)
    row_parts = peers // lane_parts
    part_rows = weight_acc.shape[0] // row_parts
    part_cols = weight_acc.shape[1] // lane_parts

    def part(r):
        return cols(lax.div(r, lane_parts), part_rows), cols(lax.rem(r, lane_parts), part_cols)

    def weight_copy(d):
        rows, columns = part(row_peer(d))
        return row_copy(weight_out.at[rows, columns], weight_in.at[me], 4, d)

    def weight_share(d):
        rows, columns = part(me)
        return row_copy(weight_sum, weight_all.at[rows, columns], 5, d)

    fill_picks(send_pick, send, 64)
    own_rows = lax.broadcasted_iota(jnp.int32, (hubs, nodes), 1)
    own_pick[...] = jnp.where(own_rows == hub_col[...], 1.0, 0.0).astype(BF16)
    hub_out[...] = dot(own_pick[...], feats[...], 1, 1).astype(BF16)

    tile = 2 * slots

    def gather_out(i, carry):
        slot_out[:, cols(i, tile)] = dot(feats[...], send_pick[:, cols(i, tile)], 1, 0).astype(BF16)
        return carry

    lax.fori_loop(0, peers * slots // tile, gather_out, 0)

    pl.semaphore_wait(barrier, peers - 1 + has_left.astype(jnp.int32) + has_right.astype(jnp.int32))
    for d in range(1, peers):
        slot_copy(d).start()
        hub_copy(d).start()
    slot_in[:, cols(me, slots)] = slot_out[:, cols(me, slots)]
    hub_in[cols(me, hubs), :] = hub_out[...]

    fill_picks(loc_pick, loc, 64)
    fill_picks(recv_pick, recv, 64)
    fill_picks(hub_pick, hub, 64)
    fixed = loc.shape[0] + hub.shape[0]

    def local_part(k, carry):
        total[k] = dot(feats[...], loc_pick[:, cols(k, width)], 1, 0)
        joined[k, 0:narrow, :] = feats[:, cols(k, width)]
        ones = jnp.ones((16, recv_pick.shape[1]), BF16)
        degree[k] = dot(ones, recv_pick[cols(k, width), :], 1, 1) + fixed
        return carry

    lax.fori_loop(0, chunks, local_part, 0)
    weight_acc[...] = jnp.zeros_like(weight_acc)
    for d in range(1, peers):
        slot_copy(d).wait_recv()
        hub_copy(d).wait_recv()

    def right_copy(owner, k):
        return pltpu.make_async_remote_copy(
            src_ref=to_right.at[k, owner], dst_ref=from_left.at[k, owner],
            send_sem=sum_send.at[0, k, owner], recv_sem=sum_recv.at[0, k, owner],
            device_id={"col": pos + 1}, device_id_type=MESH,
        )

    def left_copy(owner, k):
        return pltpu.make_async_remote_copy(
            src_ref=to_left.at[k, owner], dst_ref=from_right.at[k, owner],
            send_sem=sum_send.at[1, k, owner], recv_sem=sum_recv.at[1, k, owner],
            device_id={"col": pos - 1}, device_id_type=MESH,
        )

    def slopes_right(owner, k):
        return pltpu.make_async_remote_copy(
            src_ref=slopes.at[k, owner], dst_ref=slopes.at[k, owner],
            send_sem=spread_send.at[0, k, owner], recv_sem=spread_recv.at[0, k, owner],
            device_id={"col": pos + 1}, device_id_type=MESH,
        )

    def slopes_left(owner, k):
        return pltpu.make_async_remote_copy(
            src_ref=slopes.at[k, owner], dst_ref=slopes.at[k, owner],
            send_sem=spread_send.at[1, k, owner], recv_sem=spread_recv.at[1, k, owner],
            device_id={"col": pos - 1}, device_id_type=MESH,
        )

    def send_partials(k):
        mean = total[k] + dot(hub_in[...], hub_pick[:, cols(k, width)], 0, 0)
        mean = mean + dot(slot_in[...], recv_pick[cols(k, width), :], 1, 1)
        joined[k, narrow:, :] = (mean / degree[k, 0:1, :]).astype(BF16)

        def step(s, carry):
            far = n - 1 - s

            @pl.when(far > pos)
            def _():
                mine = dot(w_turned[far], joined[k], 1, 0)

                @pl.when(has_left)
                def _():
                    right_copy(far, k).wait_recv()
                    to_right[k, far] = (mine + from_left[k, far].astype(F32)).astype(BF16)

                @pl.when(jnp.logical_not(has_left))
                def _():
                    to_right[k, far] = mine.astype(BF16)

                right_copy(far, k).start()

            @pl.when(s < pos)
            def _():
                mine = dot(w_turned[s], joined[k], 1, 0)

                @pl.when(has_right)
                def _():
                    left_copy(s, k).wait_recv()
                    to_left[k, s] = (mine + from_right[k, s].astype(F32)).astype(BF16)

                @pl.when(jnp.logical_not(has_right))
                def _():
                    to_left[k, s] = mine.astype(BF16)

                left_copy(s, k).start()

            return carry

        lax.fori_loop(0, n - 1, step, 0)

    def finish_preact(k):
        total[k] = dot(w_turned[pos], joined[k], 1, 0)

        @pl.when(has_left)
        def _():
            right_copy(pos, k).wait_recv()
            total[k] = total[k] + from_left[k, pos].astype(F32)

        @pl.when(has_right)
        def _():
            left_copy(pos, k).wait_recv()
            total[k] = total[k] + from_right[k, pos].astype(F32)

        preact = total[k]
        gate = jax.nn.sigmoid(preact)
        slope = gate * (1.0 + preact * (1.0 - gate))
        slopes[k, pos] = (cot[:, cols(k, width)].astype(F32) * slope).astype(BF16)

        @pl.when(has_right)
        def _():
            slopes_right(pos, k).start()

        @pl.when(has_left)
        def _():
            slopes_left(pos, k).start()

        hidden[:, cols(k, width)] = (preact * gate).astype(BF16)

    def backward(k):
        def step(d, carry):
            @pl.when(pos - d >= 0)
            def _():
                slopes_right(pos - d, k).wait_recv()

                @pl.when(has_right)
                def _():
                    slopes_right(pos - d, k).start()

            @pl.when(pos + d < n)
            def _():
                slopes_left(pos + d, k).wait_recv()

                @pl.when(has_left)
                def _():
                    slopes_left(pos + d, k).start()

            return carry

        lax.fori_loop(1, n, step, 0)
        wide = slopes[k].reshape(n * narrow, width)
        back = dot(w_neigh[...], wide, 1, 0)
        share[:, cols(k, width)] = (back / degree[k, 0:1, :]).astype(BF16)
        direct[k] = dot(w_self[...], wide, 1, 0)
        weight_acc[...] += dot(joined[k], wide, 1, 1)

    def turn(t, carry):
        @pl.when(t < chunks)
        def _():
            send_partials(t)

        @pl.when(jnp.logical_and(t >= 1, t <= chunks))
        def _():
            finish_preact(t - 1)

        @pl.when(t >= 2)
        def _():
            backward(t - 2)

        return carry

    lax.fori_loop(0, chunks + 2, turn, 0)

    def back_slots(i, carry):
        back_out[:, cols(i, tile)] = dot(share[...], recv_pick[:, cols(i, tile)], 1, 0).astype(BF16)
        return carry

    lax.fori_loop(0, peers * slots // tile, back_slots, 0)
    hub_back_out[...] = dot(hub_pick[...], share[...], 1, 1)
    for d in range(1, peers):
        back_copy(d).start()
        hub_back_copy(d).start()
    weight_out[...] = weight_acc[...].astype(BF16)
    for d in range(1, peers):
        weight_copy(d).start()
    back_in[:, cols(me, slots)] = back_out[:, cols(me, slots)]
    hub_back_in[me] = hub_back_out[cols(me, hubs), :]
    my_rows, my_cols = part(me)
    weight_in[me] = weight_out[my_rows, my_cols]

    def local_back(k, carry):
        direct[k] = direct[k] + dot(share[...], loc_pick[cols(k, width), :], 1, 1)
        return carry

    lax.fori_loop(0, chunks, local_back, 0)
    for d in range(1, peers):
        back_copy(d).wait_recv()
        hub_back_copy(d).wait_recv()
    hub_total = hub_back_in[0]
    for r in range(1, peers):
        hub_total = hub_total + hub_back_in[r]
    hub_high = hub_total.astype(BF16)
    hub_low = (hub_total - hub_high.astype(F32)).astype(BF16)

    for d in range(1, peers):
        weight_copy(d).wait_recv()
    sums = weight_in[0].astype(F32)
    for r in range(1, peers):
        sums = sums + weight_in[r].astype(F32)
    weight_sum[...] = sums.astype(BF16)
    for d in range(1, peers):
        weight_share(d).start()
    weight_all[my_rows, my_cols] = weight_sum[...]

    def finish_grad(k, carry):
        grad = direct[k] + dot(back_in[...], send_pick[cols(k, width), :], 1, 1)
        grad = grad + dot(hub_high, own_pick[:, cols(k, width)], 0, 0)
        grad = grad + dot(hub_low, own_pick[:, cols(k, width)], 0, 0)
        grad_feats[:, cols(k, width)] = grad.astype(BF16)
        return carry

    lax.fori_loop(0, chunks, finish_grad, 0)
    for d in range(1, peers):
        weight_share(d).wait_recv()
    grad_self[...] = weight_all[0:narrow, :].astype(F32)
    grad_neigh[...] = weight_all[narrow:, :].astype(F32)

    for d in range(1, peers):
        slot_copy(d).wait_send()
        hub_copy(d).wait_send()
        back_copy(d).wait_send()
        hub_back_copy(d).wait_send()
        weight_copy(d).wait_send()
        weight_share(d).wait_send()

    def drain(i, carry):
        k = lax.div(i, n)
        owner = lax.rem(i, n)

        @pl.when(owner > pos)
        def _():
            right_copy(owner, k).wait_send()

        @pl.when(owner < pos)
        def _():
            left_copy(owner, k).wait_send()

        @pl.when(jnp.logical_and(owner <= pos, has_right))
        def _():
            slopes_right(owner, k).wait_send()

        @pl.when(jnp.logical_and(owner >= pos, has_left))
        def _():
            slopes_left(owner, k).wait_send()

        return carry

    lax.fori_loop(0, chunks * n, drain, 0)


def per_device(n, peers, feats, w_self, w_neigh, cotangent, loc_nbr, send_rows, recv_node, hub_rows, hub_nbr):
    narrow, nodes = feats.shape
    chunks = 4
    width = nodes // chunks
    full = w_self.shape[1]
    hubs = hub_rows.shape[0]
    every = peers * send_rows.shape[2]
    weights = jnp.concatenate([w_self, w_neigh], axis=0)
    w_turned = weights.T.reshape(n, narrow, 2 * narrow)
    lane_parts = min(peers, full // 128)
    piece = (2 * narrow * lane_parts // peers, full // lane_parts)
    vmem = pltpu.VMEM
    out = jax.ShapeDtypeStruct
    return pl.pallas_call(
        functools.partial(layer_kernel, n, peers, chunks),
        out_shape=(
            out((narrow, nodes), BF16), out((narrow, nodes), BF16),
            out((narrow, full), F32), out((narrow, full), F32),
        ),
        in_specs=[pl.BlockSpec(memory_space=vmem)] * 10,
        out_specs=[pl.BlockSpec(memory_space=vmem)] * 4,
        scratch_shapes=[
            vmem((nodes, nodes), BF16), vmem((nodes, every), BF16), vmem((nodes, every), BF16),
            vmem((peers * hubs, nodes), BF16), vmem((hubs, nodes), BF16), vmem((chunks, 16, width), F32),
            vmem((narrow, every), BF16), vmem((narrow, every), BF16),
            vmem((hubs, narrow), BF16), vmem((peers * hubs, narrow), BF16),
            vmem((chunks, narrow, width), F32), vmem((chunks, 2 * narrow, width), BF16),
            vmem((chunks, n, narrow, width), BF16), vmem((chunks, n, narrow, width), BF16),
            vmem((chunks, n, narrow, width), BF16), vmem((chunks, n, narrow, width), BF16),
            vmem((chunks, n, narrow, width), BF16),
            vmem((chunks, narrow, width), F32), vmem((narrow, nodes), BF16),
            vmem((2 * narrow, full), F32), vmem((2 * narrow, full), BF16), vmem((peers,) + piece, BF16),
            vmem(piece, BF16), vmem((2 * narrow, full), BF16),
            vmem((narrow, every), BF16), vmem((narrow, every), BF16),
            vmem((peers * hubs, narrow), F32), vmem((peers, hubs, narrow), F32),
            pltpu.SemaphoreType.DMA((6, peers)), pltpu.SemaphoreType.DMA((6, peers)),
            pltpu.SemaphoreType.DMA((2, chunks, n)), pltpu.SemaphoreType.DMA((2, chunks, n)),
            pltpu.SemaphoreType.DMA((2, chunks, n)), pltpu.SemaphoreType.DMA((2, chunks, n)),
        ],
        compiler_params=pltpu.CompilerParams(
            collective_id=0, has_side_effects=True, vmem_limit_bytes=60 * 1024 * 1024
        ),
    )(
        feats, w_self, w_neigh, w_turned, cotangent, loc_nbr.T, send_rows.reshape(1, -1),
        recv_node.reshape(1, -1), hub_rows.reshape(-1, 1), hub_nbr.T,
    )


def solution(mesh):
    return jax.shard_map(
        functools.partial(per_device, mesh.shape["col"], mesh.shape["row"]),
        mesh=mesh,
        in_specs=(
            P("col", "row"),
            P("col", None),
            P("col", None),
            P("col", "row"),
            P("row", None),
            P("row", None, None),
            P("row", None, None),
            P("row"),
            P("row", None),
        ),
        out_specs=(P("col", "row"), P("col", "row"), P("col", None), P("col", None)),
        check_vma=False,
    )
```

```python
import functools

import jax
import jax.numpy as jnp
from jax import lax
from jax.experimental import pallas as pl
from jax.experimental.pallas import tpu as pltpu
from jax.sharding import PartitionSpec as P

BF16 = jnp.bfloat16
F32 = jnp.float32
MESH = pl.DeviceIdType.MESH


def dot(a, b, ca, cb):
    return lax.dot_general(a, b, (((ca,), (cb,)), ((), ())), preferred_element_type=F32)


def fill_picks(dest, indices, strip):
    size = dest.shape[0]
    strip = min(strip, size)

    def body(i, carry):
        first = pl.multiple_of(i * strip, strip)
        rows = lax.broadcasted_iota(jnp.int32, (strip, indices.shape[1]), 0) + first
        total = jnp.where(rows == indices[0:1, :], 1.0, 0.0)
        for k in range(1, indices.shape[0]):
            total = total + jnp.where(rows == indices[k : k + 1, :], 1.0, 0.0)
        dest[pl.ds(first, strip), :] = total.astype(BF16)
        return carry

    lax.fori_loop(0, size // strip, body, 0)


def layer_kernel(
    n, peers, chunks,
    feats, w_self, w_neigh, cot, loc, send, recv, hub_row, hub,
    hidden, grad_feats, weight_all,
    loc_pick, send_pick, recv_pick, hub_pick, own_pick, degree,
    slot_out, slot_in, hub_out, hub_in,
    w_turned, partial, total, joined, from_left, from_right, to_left, to_right, slopes,
    direct, share, weight_acc, weight_out, weight_in, weight_sum,
    back_out, back_in, hub_back_out, hub_back_in,
    row_send, row_recv, sum_send, sum_recv, spread_send, spread_recv,
):
    narrow, nodes = feats.shape
    width = nodes // chunks
    slots = send.shape[1] // peers
    hubs = hub_row.shape[1]
    me = lax.axis_index("row")
    pos = lax.axis_index("col")
    has_left = pos > 0
    has_right = pos < n - 1

    def row_peer(d):
        return lax.rem(me + d, peers)

    def row_source(d):
        return lax.rem(me + peers - d, peers)

    barrier = pltpu.get_barrier_semaphore()
    for d in range(1, peers):
        pl.semaphore_signal(barrier, inc=1, device_id={"row": row_peer(d)}, device_id_type=MESH)

    @pl.when(has_left)
    def _():
        pl.semaphore_signal(barrier, inc=1, device_id={"col": pos - 1}, device_id_type=MESH)

    @pl.when(has_right)
    def _():
        pl.semaphore_signal(barrier, inc=1, device_id={"col": pos + 1}, device_id_type=MESH)

    def cols(index, size):
        return pl.ds(pl.multiple_of(index * size, size), size)

    def row_copy(src, dst, kind, d):
        return pltpu.make_async_remote_copy(
            src_ref=src, dst_ref=dst, send_sem=row_send.at[kind, d], recv_sem=row_recv.at[kind, d],
            device_id={"row": row_peer(d)}, device_id_type=MESH,
        )

    def slot_copy(d):
        return row_copy(slot_out.at[:, cols(row_peer(d), slots)], slot_in.at[:, cols(me, slots)], 0, d)

    def hub_copy(d):
        return row_copy(hub_out, hub_in.at[cols(me, hubs), :], 1, d)

    def back_copy(d):
        return row_copy(back_out.at[:, cols(row_peer(d), slots)], back_in.at[:, cols(me, slots)], 2, d)

    def hub_back_copy(d):
        return row_copy(hub_back_out.at[cols(row_peer(d), hubs), :], hub_back_in.at[me], 3, d)

    lane_parts = min(peers, weight_acc.shape[1] // 128)
    row_parts = peers // lane_parts
    part_rows = weight_acc.shape[0] // row_parts
    part_cols = weight_acc.shape[1] // lane_parts

    def part(r):
        return cols(lax.div(r, lane_parts), part_rows), cols(lax.rem(r, lane_parts), part_cols)

    def weight_copy(d):
        rows, columns = part(row_peer(d))
        return row_copy(weight_out.at[rows, columns], weight_in.at[me], 4, d)

    def weight_share(d):
        rows, columns = part(me)
        return row_copy(weight_sum, weight_all.at[rows, columns], 5, d)

    fill_picks(send_pick, send, 64)
    fill_picks(own_pick, hub_row, 64)
    hub_out[...] = dot(feats[...], own_pick[...], 1, 0).T.astype(BF16)

    tile = 2 * slots

    def gather_out(i, carry):
        slot_out[:, cols(i, tile)] = dot(feats[...], send_pick[:, cols(i, tile)], 1, 0).astype(BF16)
        return carry

    lax.fori_loop(0, peers * slots // tile, gather_out, 0)

    pl.semaphore_wait(barrier, peers - 1 + has_left.astype(jnp.int32) + has_right.astype(jnp.int32))
    for d in range(1, peers):
        slot_copy(d).start()
        hub_copy(d).start()
    slot_in[:, cols(me, slots)] = slot_out[:, cols(me, slots)]
    hub_in[cols(me, hubs), :] = hub_out[...]

    fill_picks(loc_pick, loc, 64)
    fill_picks(recv_pick, recv, 64)
    fill_picks(hub_pick, hub, 64)
    fixed = loc.shape[0] + hub.shape[0]

    pair = 2 * width

    def local_part(k, carry):
        near = dot(feats[...], loc_pick[:, cols(k, pair)], 1, 0)
        ones = jnp.ones((16, recv_pick.shape[1]), BF16)
        count = dot(ones, recv_pick[cols(k, pair), :], 1, 1) + fixed
        for half in range(2):
            there = slice(half * width, (half + 1) * width)
            total[2 * k + half] = near[:, there]
            degree[2 * k + half] = count[:, there]
            joined[2 * k + half, 0:narrow, :] = feats[:, cols(2 * k + half, width)]
        return carry

    lax.fori_loop(0, chunks // 2, local_part, 0)
    w_turned[:, 0:narrow] = w_self[...].T
    w_turned[:, narrow:] = w_neigh[...].T
    weight_acc[...] = jnp.zeros_like(weight_acc)
    for d in range(1, peers):
        slot_copy(d).wait_recv()
        hub_copy(d).wait_recv()

    def right_copy(owner, k):
        return pltpu.make_async_remote_copy(
            src_ref=to_right.at[k, owner], dst_ref=from_left.at[k, owner],
            send_sem=sum_send.at[0, k, owner], recv_sem=sum_recv.at[0, k, owner],
            device_id={"col": pos + 1}, device_id_type=MESH,
        )

    def left_copy(owner, k):
        return pltpu.make_async_remote_copy(
            src_ref=to_left.at[k, owner], dst_ref=from_right.at[k, owner],
            send_sem=sum_send.at[1, k, owner], recv_sem=sum_recv.at[1, k, owner],
            device_id={"col": pos - 1}, device_id_type=MESH,
        )

    def slopes_right(owner, k):
        return pltpu.make_async_remote_copy(
            src_ref=slopes.at[k, owner], dst_ref=slopes.at[k, owner],
            send_sem=spread_send.at[0, k, owner], recv_sem=spread_recv.at[0, k, owner],
            device_id={"col": pos + 1}, device_id_type=MESH,
        )

    def slopes_left(owner, k):
        return pltpu.make_async_remote_copy(
            src_ref=slopes.at[k, owner], dst_ref=slopes.at[k, owner],
            send_sem=spread_send.at[1, k, owner], recv_sem=spread_recv.at[1, k, owner],
            device_id={"col": pos - 1}, device_id_type=MESH,
        )

    def make_partials(k):
        mean = total[k] + dot(hub_in[...], hub_pick[:, cols(k, width)], 0, 0)
        mean = mean + dot(slot_in[...], recv_pick[cols(k, width), :], 1, 1)
        joined[k, narrow:, :] = (mean / degree[k, 0:1, :]).astype(BF16)
        partial[k] = dot(w_turned[...], joined[k], 1, 0).reshape(n, narrow, width)

    def sums_right(k):
        def step(s, carry):
            far = n - 1 - s

            @pl.when(jnp.logical_and(far > pos, has_left))
            def _():
                right_copy(far, k).wait_recv()
                to_right[k, far] = (partial[k, far] + from_left[k, far].astype(F32)).astype(BF16)

            @pl.when(jnp.logical_and(far > pos, jnp.logical_not(has_left)))
            def _():
                to_right[k, far] = partial[k, far].astype(BF16)

            @pl.when(far > pos)
            def _():
                right_copy(far, k).start()

            return carry

        lax.fori_loop(0, n - 1, step, 0)

    def sums_left(k):
        def step(s, carry):
            @pl.when(jnp.logical_and(s < pos, has_right))
            def _():
                left_copy(s, k).wait_recv()
                to_left[k, s] = (partial[k, s] + from_right[k, s].astype(F32)).astype(BF16)

            @pl.when(jnp.logical_and(s < pos, jnp.logical_not(has_right)))
            def _():
                to_left[k, s] = partial[k, s].astype(BF16)

            @pl.when(s < pos)
            def _():
                left_copy(s, k).start()

            return carry

        lax.fori_loop(0, n - 1, step, 0)

    def finish_preact(k):
        total[k] = partial[k, pos]

        @pl.when(has_left)
        def _():
            right_copy(pos, k).wait_recv()
            total[k] = total[k] + from_left[k, pos].astype(F32)

        @pl.when(has_right)
        def _():
            left_copy(pos, k).wait_recv()
            total[k] = total[k] + from_right[k, pos].astype(F32)

        preact = total[k]
        gate = jax.nn.sigmoid(preact)
        slope = gate * (1.0 + preact * (1.0 - gate))
        slopes[k, pos] = (cot[:, cols(k, width)].astype(F32) * slope).astype(BF16)

        @pl.when(has_right)
        def _():
            slopes_right(pos, k).start()

        @pl.when(has_left)
        def _():
            slopes_left(pos, k).start()

        hidden[:, cols(k, width)] = (preact * gate).astype(BF16)

    def pass_on(d, t):
        k = t - (n - 1) - d
        inside = jnp.logical_and(k >= 0, k < chunks)

        @pl.when(jnp.logical_and(inside, pos - d >= 0))
        def _():
            slopes_right(pos - d, k).wait_recv()

            @pl.when(has_right)
            def _():
                slopes_right(pos - d, k).start()

        @pl.when(jnp.logical_and(inside, pos + d < n))
        def _():
            slopes_left(pos + d, k).wait_recv()

            @pl.when(has_left)
            def _():
                slopes_left(pos + d, k).start()

    def backward(k):
        wide = jnp.concatenate(
            [slopes[k - 1].reshape(n * narrow, width), slopes[k].reshape(n * narrow, width)], axis=1
        )
        back = dot(w_neigh[...], wide, 1, 0)
        own = dot(w_self[...], wide, 1, 0)
        for half in range(2):
            at = k - 1 + half
            there = slice(half * width, (half + 1) * width)
            share[:, cols(at, width)] = (back[:, there] / degree[at, 0:1, :]).astype(BF16)
            direct[at] = own[:, there]
        weight_acc[...] += dot(jnp.concatenate([joined[k - 1], joined[k]], axis=1), wide, 1, 1)

    def when_inside(k, work):
        @pl.when(jnp.logical_and(k >= 0, k < chunks))
        def _():
            work(k)

    def turn(t, carry):
        def passing(d, inner):
            pass_on(d, t)
            return inner

        lax.fori_loop(1, n, passing, 0)
        when_inside(t, make_partials)
        when_inside(t - pos, sums_right)
        when_inside(t - (n - 1 - pos), sums_left)
        when_inside(t - (n - 1), finish_preact)
        late = t - 2 * (n - 1)

        @pl.when(jnp.logical_and(late >= 0, lax.rem(late, 2) == 1))
        def _():
            backward(late)

        return carry

    lax.fori_loop(0, chunks + 2 * (n - 1), turn, 0)

    def back_slots(i, carry):
        back_out[:, cols(i, tile)] = dot(share[...], recv_pick[:, cols(i, tile)], 1, 0).astype(BF16)
        return carry

    lax.fori_loop(0, peers * slots // tile, back_slots, 0)
    hub_back_out[...] = dot(hub_pick[...], share[...], 1, 1)
    for d in range(1, peers):
        back_copy(d).start()
        hub_back_copy(d).start()
    weight_out[...] = weight_acc[...].astype(BF16)
    for d in range(1, peers):
        weight_copy(d).start()
    back_in[:, cols(me, slots)] = back_out[:, cols(me, slots)]
    hub_back_in[me] = hub_back_out[cols(me, hubs), :]
    my_rows, my_cols = part(me)
    weight_in[me] = weight_out[my_rows, my_cols]

    def local_back(k, carry):
        direct[k] = direct[k] + dot(share[...], loc_pick[cols(k, width), :], 1, 1)
        return carry

    lax.fori_loop(0, chunks, local_back, 0)
    for d in range(1, peers):
        back_copy(d).wait_recv()
        hub_back_copy(d).wait_recv()
    hub_total = hub_back_in[0]
    for r in range(1, peers):
        hub_total = hub_total + hub_back_in[r]
    hub_total = hub_total.T
    hub_high = hub_total.astype(BF16)
    hub_low = (hub_total - hub_high.astype(F32)).astype(BF16)

    for d in range(1, peers):
        weight_copy(d).wait_recv()
    sums = weight_in[0].astype(F32)
    for r in range(1, peers):
        sums = sums + weight_in[r].astype(F32)
    weight_sum[...] = sums.astype(BF16)
    for d in range(1, peers):
        weight_share(d).start()
    weight_all[my_rows, my_cols] = weight_sum[...]

    def finish_grad(k, carry):
        grad = direct[k] + dot(back_in[...], send_pick[cols(k, width), :], 1, 1)
        grad = grad + dot(hub_high, own_pick[cols(k, width), :], 1, 1)
        grad = grad + dot(hub_low, own_pick[cols(k, width), :], 1, 1)
        grad_feats[:, cols(k, width)] = grad.astype(BF16)
        return carry

    lax.fori_loop(0, chunks, finish_grad, 0)
    for d in range(1, peers):
        weight_share(d).wait_recv()

    for d in range(1, peers):
        slot_copy(d).wait_send()
        hub_copy(d).wait_send()
        back_copy(d).wait_send()
        hub_back_copy(d).wait_send()
        weight_copy(d).wait_send()
        weight_share(d).wait_send()

    def drain(i, carry):
        k = lax.div(i, n)
        owner = lax.rem(i, n)

        @pl.when(owner > pos)
        def _():
            right_copy(owner, k).wait_send()

        @pl.when(owner < pos)
        def _():
            left_copy(owner, k).wait_send()

        @pl.when(jnp.logical_and(owner <= pos, has_right))
        def _():
            slopes_right(owner, k).wait_send()

        @pl.when(jnp.logical_and(owner >= pos, has_left))
        def _():
            slopes_left(owner, k).wait_send()

        return carry

    lax.fori_loop(0, chunks * n, drain, 0)


def per_device(n, peers, feats, w_self, w_neigh, cotangent, loc_nbr, send_rows, recv_node, hub_rows, hub_nbr):
    narrow, nodes = feats.shape
    chunks = 8
    width = nodes // chunks
    full = w_self.shape[1]
    hubs = hub_rows.shape[0]
    every = peers * send_rows.shape[2]
    lane_parts = min(peers, full // 128)
    piece = (2 * narrow * lane_parts // peers, full // lane_parts)
    vmem = pltpu.VMEM
    out = jax.ShapeDtypeStruct
    hidden, grad_feats, weight_all = pl.pallas_call(
        functools.partial(layer_kernel, n, peers, chunks),
        out_shape=(
            out((narrow, nodes), BF16), out((narrow, nodes), BF16),
            out((2 * narrow, full), BF16),
        ),
        in_specs=[pl.BlockSpec(memory_space=vmem)] * 9,
        out_specs=[pl.BlockSpec(memory_space=vmem)] * 3,
        scratch_shapes=[
            vmem((nodes, nodes), BF16), vmem((nodes, every), BF16), vmem((nodes, every), BF16),
            vmem((peers * hubs, nodes), BF16), vmem((nodes, hubs), BF16), vmem((chunks, 16, width), F32),
            vmem((narrow, every), BF16), vmem((narrow, every), BF16),
            vmem((hubs, narrow), BF16), vmem((peers * hubs, narrow), BF16),
            vmem((full, 2 * narrow), BF16), vmem((chunks, n, narrow, width), F32),
            vmem((chunks, narrow, width), F32), vmem((chunks, 2 * narrow, width), BF16),
            vmem((chunks, n, narrow, width), BF16), vmem((chunks, n, narrow, width), BF16),
            vmem((chunks, n, narrow, width), BF16), vmem((chunks, n, narrow, width), BF16),
            vmem((chunks, n, narrow, width), BF16),
            vmem((chunks, narrow, width), F32), vmem((narrow, nodes), BF16),
            vmem((2 * narrow, full), F32), vmem((2 * narrow, full), BF16), vmem((peers,) + piece, BF16),
            vmem(piece, BF16),
            vmem((narrow, every), BF16), vmem((narrow, every), BF16),
            vmem((peers * hubs, narrow), F32), vmem((peers, hubs, narrow), F32),
            pltpu.SemaphoreType.DMA((6, peers)), pltpu.SemaphoreType.DMA((6, peers)),
            pltpu.SemaphoreType.DMA((2, chunks, n)), pltpu.SemaphoreType.DMA((2, chunks, n)),
            pltpu.SemaphoreType.DMA((2, chunks, n)), pltpu.SemaphoreType.DMA((2, chunks, n)),
        ],
        compiler_params=pltpu.CompilerParams(
            collective_id=0, has_side_effects=True, vmem_limit_bytes=60 * 1024 * 1024
        ),
    )(
        feats, w_self, w_neigh, cotangent, loc_nbr.T, send_rows.reshape(1, -1),
        recv_node.reshape(1, -1), hub_rows.reshape(1, -1), hub_nbr.T,
    )
    grads = weight_all.astype(F32)
    return hidden, grad_feats, grads[:narrow], grads[narrow:]


def solution(mesh):
    return jax.shard_map(
        functools.partial(per_device, mesh.shape["col"], mesh.shape["row"]),
        mesh=mesh,
        in_specs=(
            P("col", "row"),
            P("col", None),
            P("col", None),
            P("col", "row"),
            P("row", None),
            P("row", None, None),
            P("row", None, None),
            P("row"),
            P("row", None),
        ),
        out_specs=(P("col", "row"), P("col", "row"), P("col", None), P("col", None)),
        check_vma=False,
    )
```

```python
import functools

import jax
import jax.numpy as jnp
from jax import lax
from jax.experimental import pallas as pl
from jax.experimental.pallas import tpu as pltpu
from jax.sharding import PartitionSpec as P

BF16 = jnp.bfloat16
F32 = jnp.float32
MESH = pl.DeviceIdType.MESH


def dot(a, b, ca, cb):
    return lax.dot_general(a, b, (((ca,), (cb,)), ((), ())), preferred_element_type=F32)


def count_picks(indices, first, rows):
    names = lax.broadcasted_iota(jnp.int32, (rows, indices.shape[1]), 0) + first
    total = jnp.where(names == indices[0:1, :], 1.0, 0.0)
    for k in range(1, indices.shape[0]):
        total = total + jnp.where(names == indices[k : k + 1, :], 1.0, 0.0)
    return total.astype(BF16)


def fill_picks(dest, indices, strip):
    strip = min(strip, dest.shape[0])

    def body(i, carry):
        first = pl.multiple_of(i * strip, strip)
        dest[pl.ds(first, strip), :] = count_picks(indices, first, strip)
        return carry

    lax.fori_loop(0, dest.shape[0] // strip, body, 0)


def layer_kernel(
    n, peers, chunks,
    feats, w_self, w_neigh, cot, loc, send, recv, hub_row, hub,
    hidden, grad_feats, weight_all,
    loc_pick, send_pick, recv_pick, hub_pick, own_pick, degree,
    slot_out, slot_in, hub_out, hub_in,
    w_turned, partial, total, joined, from_left, from_right, to_left, to_right, slopes,
    direct, share, weight_acc, weight_out, twin_in, weight_half, weight_in, weight_sum,
    back_out, back_in, hub_back_out, hub_back_in,
    row_send, row_recv, sum_send, sum_recv, spread_send, spread_recv,
):
    narrow, nodes = feats.shape
    width = nodes // chunks
    slots = send.shape[1] // peers
    hubs = hub_row.shape[1]
    me = lax.axis_index("row")
    pos = lax.axis_index("col")
    has_left = pos > 0
    has_right = pos < n - 1

    def row_peer(d):
        return lax.rem(me + d, peers)

    def row_source(d):
        return lax.rem(me + peers - d, peers)

    barrier = pltpu.get_barrier_semaphore()
    for d in range(1, peers):
        pl.semaphore_signal(barrier, inc=1, device_id={"row": row_peer(d)}, device_id_type=MESH)

    @pl.when(has_left)
    def _():
        pl.semaphore_signal(barrier, inc=1, device_id={"col": pos - 1}, device_id_type=MESH)

    @pl.when(has_right)
    def _():
        pl.semaphore_signal(barrier, inc=1, device_id={"col": pos + 1}, device_id_type=MESH)

    def cols(index, size):
        return pl.ds(pl.multiple_of(index * size, size), size)

    def row_copy(src, dst, kind, d):
        return pltpu.make_async_remote_copy(
            src_ref=src, dst_ref=dst, send_sem=row_send.at[kind, d], recv_sem=row_recv.at[kind, d],
            device_id={"row": row_peer(d)}, device_id_type=MESH,
        )

    def slot_copy(d):
        return row_copy(slot_out.at[:, cols(row_peer(d), slots)], slot_in.at[:, cols(me, slots)], 0, d)

    def hub_copy(d):
        return row_copy(hub_out, hub_in.at[cols(me, hubs), :], 1, d)

    def back_copy(d):
        return row_copy(back_out.at[:, cols(row_peer(d), slots)], back_in.at[:, cols(me, slots)], 2, d)

    def hub_back_copy(d):
        return row_copy(hub_back_out.at[cols(row_peer(d), hubs), :], hub_back_in.at[me], 3, d)

    lane_parts = min(peers, weight_acc.shape[1] // 128)
    row_parts = peers // lane_parts
    part_rows = weight_acc.shape[0] // row_parts
    part_cols = weight_acc.shape[1] // lane_parts

    def part(r):
        return cols(lax.div(r, lane_parts), part_rows), cols(lax.rem(r, lane_parts), part_cols)

    chips = peers // 2
    chip = lax.div(me, 2)
    core = lax.rem(me, 2)
    twin = me + 1 - 2 * core

    def other_chip(d):
        return lax.rem(chip + d, chips)

    def to_row(src, dst, kind, index, peer):
        return pltpu.make_async_remote_copy(
            src_ref=src, dst_ref=dst, send_sem=row_send.at[kind, index], recv_sem=row_recv.at[kind, index],
            device_id={"row": peer}, device_id_type=MESH,
        )

    def twin_copy(c):
        rows, columns = part(2 * c + 1 - core)
        return to_row(weight_out.at[rows, columns], twin_in.at[c], 4, c, twin)

    def weight_copy(d):
        c = other_chip(d)
        return to_row(weight_half.at[c], weight_in.at[chip], 5, d, 2 * c + core)

    def weight_share(d):
        rows, columns = part(me)
        return to_row(weight_sum, weight_all.at[rows, columns], 6, d, 2 * other_chip(d) + core)

    def weight_twin(d):
        rows, columns = part(2 * other_chip(d) + core)
        return to_row(weight_all.at[rows, columns], weight_all.at[rows, columns], 7, d, twin)

    def weight_twin_in(d):
        rows, columns = part(2 * other_chip(d) + 1 - core)
        return to_row(weight_all.at[rows, columns], weight_all.at[rows, columns], 7, d, twin)

    fill_picks(send_pick, send[...], 16)
    fill_picks(own_pick, hub_row[...], 64)
    hub_out[...] = dot(feats[...], own_pick[...], 1, 0).T.astype(BF16)

    tile = 2 * slots

    def gather_out(i, carry):
        slot_out[:, cols(i, tile)] = dot(feats[...], send_pick[:, cols(i, tile)], 1, 0).astype(BF16)
        return carry

    lax.fori_loop(0, peers * slots // tile, gather_out, 0)

    pl.semaphore_wait(barrier, peers - 1 + has_left.astype(jnp.int32) + has_right.astype(jnp.int32))
    for d in range(1, peers):
        slot_copy(d).start()
        hub_copy(d).start()
    slot_in[:, cols(me, slots)] = slot_out[:, cols(me, slots)]
    hub_in[cols(me, hubs), :] = hub_out[...]

    fixed = loc.shape[0] + hub.shape[0]

    def prepare(k):
        here = cols(k, width)
        names = loc[:, here]

        def local_rows(i, carry):
            first = pl.multiple_of(i * 128, 128)
            loc_pick[pl.ds(first, 128), here] = count_picks(names, first, 128)
            return carry

        lax.fori_loop(0, nodes // 128, local_rows, 0)
        targets = recv[...]

        def target_rows(i, carry):
            first = pl.multiple_of(k * width + i * 16, 16)
            recv_pick[pl.ds(first, 16), :] = count_picks(targets, first, 16)
            return carry

        lax.fori_loop(0, width // 16, target_rows, 0)
        hub_pick[:, here] = count_picks(hub[:, here], 0, hub_pick.shape[0])
        total[k] = dot(feats[...], loc_pick[:, here], 1, 0)
        ones = jnp.ones((16, recv_pick.shape[1]), BF16)
        degree[k] = dot(ones, recv_pick[here, :], 1, 1) + fixed
        joined[k, 0:narrow, :] = feats[:, here]

    prepare(0)
    prepare(1)
    w_turned[:, 0:narrow] = w_self[...].T
    w_turned[:, narrow:] = w_neigh[...].T
    weight_acc[...] = jnp.zeros_like(weight_acc)
    for d in range(1, peers):
        slot_copy(d).wait_recv()
        hub_copy(d).wait_recv()

    def right_copy(owner, k):
        return pltpu.make_async_remote_copy(
            src_ref=to_right.at[k, owner], dst_ref=from_left.at[k, owner],
            send_sem=sum_send.at[0, k, owner], recv_sem=sum_recv.at[0, k, owner],
            device_id={"col": pos + 1}, device_id_type=MESH,
        )

    def left_copy(owner, k):
        return pltpu.make_async_remote_copy(
            src_ref=to_left.at[k, owner], dst_ref=from_right.at[k, owner],
            send_sem=sum_send.at[1, k, owner], recv_sem=sum_recv.at[1, k, owner],
            device_id={"col": pos - 1}, device_id_type=MESH,
        )

    def slopes_right(owner, k):
        return pltpu.make_async_remote_copy(
            src_ref=slopes.at[k, owner], dst_ref=slopes.at[k, owner],
            send_sem=spread_send.at[0, k, owner], recv_sem=spread_recv.at[0, k, owner],
            device_id={"col": pos + 1}, device_id_type=MESH,
        )

    def slopes_left(owner, k):
        return pltpu.make_async_remote_copy(
            src_ref=slopes.at[k, owner], dst_ref=slopes.at[k, owner],
            send_sem=spread_send.at[1, k, owner], recv_sem=spread_recv.at[1, k, owner],
            device_id={"col": pos - 1}, device_id_type=MESH,
        )

    def make_partials(k):
        mean = total[k] + dot(hub_in[...], hub_pick[:, cols(k, width)], 0, 0)
        mean = mean + dot(slot_in[...], recv_pick[cols(k, width), :], 1, 1)
        joined[k, narrow:, :] = (mean / degree[k, 0:1, :]).astype(BF16)
        partial[k] = dot(w_turned[...], joined[k], 1, 0).reshape(n, narrow, width)

    def sums_right(k):
        def step(s, carry):
            far = n - 1 - s

            @pl.when(jnp.logical_and(far > pos, has_left))
            def _():
                right_copy(far, k).wait_recv()
                to_right[k, far] = (partial[k, far] + from_left[k, far].astype(F32)).astype(BF16)

            @pl.when(jnp.logical_and(far > pos, jnp.logical_not(has_left)))
            def _():
                to_right[k, far] = partial[k, far].astype(BF16)

            @pl.when(far > pos)
            def _():
                right_copy(far, k).start()

            return carry

        lax.fori_loop(0, n - 1, step, 0)

    def sums_left(k):
        def step(s, carry):
            @pl.when(jnp.logical_and(s < pos, has_right))
            def _():
                left_copy(s, k).wait_recv()
                to_left[k, s] = (partial[k, s] + from_right[k, s].astype(F32)).astype(BF16)

            @pl.when(jnp.logical_and(s < pos, jnp.logical_not(has_right)))
            def _():
                to_left[k, s] = partial[k, s].astype(BF16)

            @pl.when(s < pos)
            def _():
                left_copy(s, k).start()

            return carry

        lax.fori_loop(0, n - 1, step, 0)

    def finish_preact(k):
        total[k] = partial[k, pos]

        @pl.when(has_left)
        def _():
            right_copy(pos, k).wait_recv()
            total[k] = total[k] + from_left[k, pos].astype(F32)

        @pl.when(has_right)
        def _():
            left_copy(pos, k).wait_recv()
            total[k] = total[k] + from_right[k, pos].astype(F32)

        preact = total[k]
        gate = jax.nn.sigmoid(preact)
        slope = gate * (1.0 + preact * (1.0 - gate))
        slopes[k, pos] = (cot[:, cols(k, width)].astype(F32) * slope).astype(BF16)

        @pl.when(has_right)
        def _():
            slopes_right(pos, k).start()

        @pl.when(has_left)
        def _():
            slopes_left(pos, k).start()

        hidden[:, cols(k, width)] = (preact * gate).astype(BF16)

    def pass_on(d, t):
        k = t - (n - 1) - d
        inside = jnp.logical_and(k >= 0, k < chunks)

        @pl.when(jnp.logical_and(inside, pos - d >= 0))
        def _():
            slopes_right(pos - d, k).wait_recv()

            @pl.when(has_right)
            def _():
                slopes_right(pos - d, k).start()

        @pl.when(jnp.logical_and(inside, pos + d < n))
        def _():
            slopes_left(pos + d, k).wait_recv()

            @pl.when(has_left)
            def _():
                slopes_left(pos + d, k).start()

    def backward(k):
        wide = jnp.concatenate(
            [slopes[k - 1].reshape(n * narrow, width), slopes[k].reshape(n * narrow, width)], axis=1
        )
        back = dot(w_neigh[...], wide, 1, 0)
        own = dot(w_self[...], wide, 1, 0)
        for half in range(2):
            at = k - 1 + half
            there = slice(half * width, (half + 1) * width)
            share[:, cols(at, width)] = (back[:, there] / degree[at, 0:1, :]).astype(BF16)
            direct[at] = own[:, there]
        weight_acc[...] += dot(jnp.concatenate([joined[k - 1], joined[k]], axis=1), wide, 1, 1)

    def when_inside(k, work):
        @pl.when(jnp.logical_and(k >= 0, k < chunks))
        def _():
            work(k)

    def turn(t, carry):
        def passing(d, inner):
            pass_on(d, t)
            return inner

        when_inside(t, make_partials)
        lax.fori_loop(1, n, passing, 0)
        when_inside(t - pos, sums_right)
        when_inside(t - (n - 1 - pos), sums_left)
        when_inside(t - (n - 1), finish_preact)

        @pl.when(t + 2 < chunks)
        def _():
            prepare(t + 2)

        late = t - 2 * (n - 1)

        @pl.when(jnp.logical_and(late >= 0, lax.rem(late, 2) == 1))
        def _():
            backward(late)

        return carry

    lax.fori_loop(0, chunks + 2 * (n - 1), turn, 0)

    weight_out[...] = weight_acc[...].astype(BF16)
    for c in range(chips):
        twin_copy(c).start()
    def back_slots(i, carry):
        back_out[:, cols(i, tile)] = dot(share[...], recv_pick[:, cols(i, tile)], 1, 0).astype(BF16)
        return carry

    lax.fori_loop(0, peers * slots // tile, back_slots, 0)
    for d in range(1, peers):
        back_copy(d).start()
    hub_back_out[...] = dot(hub_pick[...], share[...], 1, 1)
    for d in range(1, peers):
        hub_back_copy(d).start()
    back_in[:, cols(me, slots)] = back_out[:, cols(me, slots)]
    hub_back_in[me] = hub_back_out[cols(me, hubs), :]
    for c in range(chips):
        twin_copy(c).wait_recv()
        rows, columns = part(2 * c + core)
        weight_half[c] = (weight_acc[rows, columns] + twin_in[c].astype(F32)).astype(BF16)
    for d in range(1, chips):
        weight_copy(d).start()

    def local_back(k, carry):
        direct[k] = direct[k] + dot(share[...], loc_pick[cols(k, width), :], 1, 1)
        return carry

    lax.fori_loop(0, chunks, local_back, 0)
    for d in range(1, peers):
        back_copy(d).wait_recv()
        hub_back_copy(d).wait_recv()
    hub_total = hub_back_in[0]
    for r in range(1, peers):
        hub_total = hub_total + hub_back_in[r]
    hub_total = hub_total.T
    hub_high = hub_total.astype(BF16)
    hub_low = (hub_total - hub_high.astype(F32)).astype(BF16)

    my_rows, my_cols = part(me)
    sums = weight_acc[my_rows, my_cols] + twin_in[chip].astype(F32)
    for d in range(1, chips):
        weight_copy(d).wait_recv()
        sums = sums + weight_in[lax.rem(chip + chips - d, chips)].astype(F32)
    weight_sum[...] = sums.astype(BF16)
    for d in range(1, chips):
        weight_share(d).start()
    weight_all[my_rows, my_cols] = weight_sum[...]
    weight_twin(0).start()

    def finish_grad(k, carry):
        grad = direct[k] + dot(back_in[...], send_pick[cols(k, width), :], 1, 1)
        grad = grad + dot(hub_high, own_pick[cols(k, width), :], 1, 1)
        grad = grad + dot(hub_low, own_pick[cols(k, width), :], 1, 1)
        grad_feats[:, cols(k, width)] = grad.astype(BF16)
        return carry

    lax.fori_loop(0, chunks, finish_grad, 0)
    def source_chip(d):
        return chips - d if d else 0

    for d in range(1, chips):
        weight_share(d).wait_recv()
        weight_twin(source_chip(d)).start()
    for d in range(chips):
        weight_twin_in(d).wait_recv()

    for d in range(1, peers):
        slot_copy(d).wait_send()
        hub_copy(d).wait_send()
        back_copy(d).wait_send()
        hub_back_copy(d).wait_send()
    for d in range(chips):
        twin_copy(d).wait_send()
        weight_twin(d).wait_send()
    for d in range(1, chips):
        weight_copy(d).wait_send()
        weight_share(d).wait_send()

    def drain(i, carry):
        k = lax.div(i, n)
        owner = lax.rem(i, n)

        @pl.when(owner > pos)
        def _():
            right_copy(owner, k).wait_send()

        @pl.when(owner < pos)
        def _():
            left_copy(owner, k).wait_send()

        @pl.when(jnp.logical_and(owner <= pos, has_right))
        def _():
            slopes_right(owner, k).wait_send()

        @pl.when(jnp.logical_and(owner >= pos, has_left))
        def _():
            slopes_left(owner, k).wait_send()

        return carry

    lax.fori_loop(0, chunks * n, drain, 0)


def per_device(n, peers, feats, w_self, w_neigh, cotangent, loc_nbr, send_rows, recv_node, hub_rows, hub_nbr):
    narrow, nodes = feats.shape
    chunks = 8
    width = nodes // chunks
    full = w_self.shape[1]
    hubs = hub_rows.shape[0]
    every = peers * send_rows.shape[2]
    lane_parts = min(peers, full // 128)
    piece = (2 * narrow * lane_parts // peers, full // lane_parts)
    vmem = pltpu.VMEM
    out = jax.ShapeDtypeStruct
    hidden, grad_feats, weight_all = pl.pallas_call(
        functools.partial(layer_kernel, n, peers, chunks),
        out_shape=(
            out((narrow, nodes), BF16), out((narrow, nodes), BF16),
            out((2 * narrow, full), BF16),
        ),
        in_specs=[pl.BlockSpec(memory_space=vmem)] * 9,
        out_specs=[pl.BlockSpec(memory_space=vmem)] * 3,
        scratch_shapes=[
            vmem((nodes, nodes), BF16), vmem((nodes, every), BF16), vmem((nodes, every), BF16),
            vmem((peers * hubs, nodes), BF16), vmem((nodes, hubs), BF16), vmem((chunks, 16, width), F32),
            vmem((narrow, every), BF16), vmem((narrow, every), BF16),
            vmem((hubs, narrow), BF16), vmem((peers * hubs, narrow), BF16),
            vmem((full, 2 * narrow), BF16), vmem((chunks, n, narrow, width), F32),
            vmem((chunks, narrow, width), F32), vmem((chunks, 2 * narrow, width), BF16),
            vmem((chunks, n, narrow, width), BF16), vmem((chunks, n, narrow, width), BF16),
            vmem((chunks, n, narrow, width), BF16), vmem((chunks, n, narrow, width), BF16),
            vmem((chunks, n, narrow, width), BF16),
            vmem((chunks, narrow, width), F32), vmem((narrow, nodes), BF16),
            vmem((2 * narrow, full), F32), vmem((2 * narrow, full), BF16), vmem((peers // 2,) + piece, BF16),
            vmem((peers // 2,) + piece, BF16), vmem((peers // 2,) + piece, BF16),
            vmem(piece, BF16),
            vmem((narrow, every), BF16), vmem((narrow, every), BF16),
            vmem((peers * hubs, narrow), F32), vmem((peers, hubs, narrow), F32),
            pltpu.SemaphoreType.DMA((8, peers)), pltpu.SemaphoreType.DMA((8, peers)),
            pltpu.SemaphoreType.DMA((2, chunks, n)), pltpu.SemaphoreType.DMA((2, chunks, n)),
            pltpu.SemaphoreType.DMA((2, chunks, n)), pltpu.SemaphoreType.DMA((2, chunks, n)),
        ],
        compiler_params=pltpu.CompilerParams(
            collective_id=0, has_side_effects=True, vmem_limit_bytes=60 * 1024 * 1024
        ),
    )(
        feats, w_self, w_neigh, cotangent, loc_nbr.T, send_rows.reshape(1, -1),
        recv_node.reshape(1, -1), hub_rows.reshape(1, -1), hub_nbr.T,
    )
    grads = weight_all.astype(F32)
    return hidden, grad_feats, grads[:narrow], grads[narrow:]


def solution(mesh):
    return jax.shard_map(
        functools.partial(per_device, mesh.shape["col"], mesh.shape["row"]),
        mesh=mesh,
        in_specs=(
            P("col", "row"),
            P("col", None),
            P("col", None),
            P("col", "row"),
            P("row", None),
            P("row", None, None),
            P("row", None, None),
            P("row"),
            P("row", None),
        ),
        out_specs=(P("col", "row"), P("col", "row"), P("col", None), P("col", None)),
        check_vma=False,
    )
```

```python
import functools

import jax
import jax.numpy as jnp
from jax import lax
from jax.experimental import pallas as pl
from jax.experimental.pallas import tpu as pltpu
from jax.sharding import PartitionSpec as P

BF16 = jnp.bfloat16
F32 = jnp.float32
MESH = pl.DeviceIdType.MESH


def dot(a, b, ca, cb):
    return lax.dot_general(a, b, (((ca,), (cb,)), ((), ())), preferred_element_type=F32)


def count_picks(indices, first, rows):
    names = lax.broadcasted_iota(jnp.int32, (rows, indices.shape[1]), 0) + first
    total = jnp.where(names == indices[0:1, :], 1.0, 0.0)
    for k in range(1, indices.shape[0]):
        total = total + jnp.where(names == indices[k : k + 1, :], 1.0, 0.0)
    return total.astype(BF16)


def fill_picks(dest, indices, strip):
    strip = min(strip, dest.shape[0])

    def body(i, carry):
        first = pl.multiple_of(i * strip, strip)
        dest[pl.ds(first, strip), :] = count_picks(indices, first, strip)
        return carry

    lax.fori_loop(0, dest.shape[0] // strip, body, 0)


def layer_kernel(
    n, peers, chunks,
    feats, w_self, w_neigh, cot, loc, send, recv, hub_row, hub,
    hidden, grad_feats, weight_all,
    loc_pick, send_pick, recv_pick, hub_pick, own_pick, degree,
    slot_out, slot_in, hub_out, hub_in,
    w_turned, partial, total, joined, from_left, from_right, to_left, to_right, slopes,
    direct, share, weight_acc, weight_out, twin_in, weight_half, weight_in, weight_sum,
    back_out, back_in, hub_back_out, hub_back_in,
    row_send, row_recv, sum_send, sum_recv, spread_send, spread_recv,
):
    narrow, nodes = feats.shape
    width = nodes // chunks
    slots = send.shape[1] // peers
    hubs = hub_row.shape[1]
    me = lax.axis_index("row")
    pos = lax.axis_index("col")
    has_left = pos > 0
    has_right = pos < n - 1

    def row_peer(d):
        return lax.rem(me + d, peers)

    def row_source(d):
        return lax.rem(me + peers - d, peers)

    barrier = pltpu.get_barrier_semaphore()
    for d in range(1, peers):
        pl.semaphore_signal(barrier, inc=1, device_id={"row": row_peer(d)}, device_id_type=MESH)

    @pl.when(has_left)
    def _():
        pl.semaphore_signal(barrier, inc=1, device_id={"col": pos - 1}, device_id_type=MESH)

    @pl.when(has_right)
    def _():
        pl.semaphore_signal(barrier, inc=1, device_id={"col": pos + 1}, device_id_type=MESH)

    def cols(index, size):
        return pl.ds(pl.multiple_of(index * size, size), size)

    def row_copy(src, dst, kind, d):
        return pltpu.make_async_remote_copy(
            src_ref=src, dst_ref=dst, send_sem=row_send.at[kind, d], recv_sem=row_recv.at[kind, d],
            device_id={"row": row_peer(d)}, device_id_type=MESH,
        )

    def slot_copy(d):
        return row_copy(slot_out.at[:, cols(row_peer(d), slots)], slot_in.at[:, cols(me, slots)], 0, d)

    def hub_copy(d):
        return row_copy(hub_out, hub_in.at[cols(me, hubs), :], 1, d)

    def back_copy(d):
        return row_copy(back_out.at[:, cols(row_peer(d), slots)], back_in.at[:, cols(me, slots)], 2, d)

    def hub_back_copy(d):
        return row_copy(hub_back_out.at[cols(row_peer(d), hubs), :], hub_back_in.at[me], 3, d)

    lane_parts = min(peers, weight_acc.shape[1] // 128)
    row_parts = peers // lane_parts
    part_rows = weight_acc.shape[0] // row_parts
    part_cols = weight_acc.shape[1] // lane_parts

    def part(r):
        return cols(lax.div(r, lane_parts), part_rows), cols(lax.rem(r, lane_parts), part_cols)

    chips = peers // 2
    chip = lax.div(me, 2)
    core = lax.rem(me, 2)
    twin = me + 1 - 2 * core

    def other_chip(d):
        return lax.rem(chip + d, chips)

    def to_row(src, dst, kind, index, peer):
        return pltpu.make_async_remote_copy(
            src_ref=src, dst_ref=dst, send_sem=row_send.at[kind, index], recv_sem=row_recv.at[kind, index],
            device_id={"row": peer}, device_id_type=MESH,
        )

    def twin_copy(c):
        rows, columns = part(2 * c + 1 - core)
        return to_row(weight_out.at[rows, columns], twin_in.at[c], 4, c, twin)

    def weight_copy(d):
        c = other_chip(d)
        return to_row(weight_half.at[c], weight_in.at[chip], 5, d, 2 * c + core)

    def weight_share(d):
        rows, columns = part(me)
        return to_row(weight_sum, weight_all.at[rows, columns], 6, d, 2 * other_chip(d) + core)

    def weight_twin(d):
        rows, columns = part(2 * other_chip(d) + core)
        return to_row(weight_all.at[rows, columns], weight_all.at[rows, columns], 7, d, twin)

    def weight_twin_in(d):
        rows, columns = part(2 * other_chip(d) + 1 - core)
        return to_row(weight_all.at[rows, columns], weight_all.at[rows, columns], 7, d, twin)

    fill_picks(send_pick, send[...], 16)
    fill_picks(own_pick, hub_row[...], 64)
    hub_out[...] = dot(feats[...], own_pick[...], 1, 0).T.astype(BF16)

    tile = 2 * slots

    def gather_out(i, carry):
        slot_out[:, cols(i, tile)] = dot(feats[...], send_pick[:, cols(i, tile)], 1, 0).astype(BF16)
        return carry

    lax.fori_loop(0, peers * slots // tile, gather_out, 0)

    pl.semaphore_wait(barrier, peers - 1 + has_left.astype(jnp.int32) + has_right.astype(jnp.int32))
    for d in range(1, peers):
        slot_copy(d).start()
        hub_copy(d).start()
    slot_in[:, cols(me, slots)] = slot_out[:, cols(me, slots)]
    hub_in[cols(me, hubs), :] = hub_out[...]

    fixed = loc.shape[0] + hub.shape[0]

    def prepare(k):
        here = cols(k, width)
        names = loc[:, here]

        def local_rows(i, carry):
            first = pl.multiple_of(i * 128, 128)
            loc_pick[pl.ds(first, 128), here] = count_picks(names, first, 128)
            return carry

        lax.fori_loop(0, nodes // 128, local_rows, 0)
        targets = recv[...]

        def target_rows(i, carry):
            first = pl.multiple_of(k * width + i * 16, 16)
            recv_pick[pl.ds(first, 16), :] = count_picks(targets, first, 16)
            return carry

        lax.fori_loop(0, width // 16, target_rows, 0)
        hub_pick[:, here] = count_picks(hub[:, here], 0, hub_pick.shape[0])
        total[k] = dot(feats[...], loc_pick[:, here], 1, 0)
        ones = jnp.ones((16, recv_pick.shape[1]), BF16)
        degree[k] = dot(ones, recv_pick[here, :], 1, 1) + fixed
        joined[k, 0:narrow, :] = feats[:, here]

    prepare(0)
    prepare(1)
    w_turned[:, 0:narrow] = w_self[...].T
    w_turned[:, narrow:] = w_neigh[...].T
    weight_acc[...] = jnp.zeros_like(weight_acc)
    for d in range(1, peers):
        slot_copy(d).wait_recv()
        hub_copy(d).wait_recv()

    def right_copy(owner, k):
        return pltpu.make_async_remote_copy(
            src_ref=to_right.at[k, owner], dst_ref=from_left.at[k, owner],
            send_sem=sum_send.at[0, k, owner], recv_sem=sum_recv.at[0, k, owner],
            device_id={"col": pos + 1}, device_id_type=MESH,
        )

    def left_copy(owner, k):
        return pltpu.make_async_remote_copy(
            src_ref=to_left.at[k, owner], dst_ref=from_right.at[k, owner],
            send_sem=sum_send.at[1, k, owner], recv_sem=sum_recv.at[1, k, owner],
            device_id={"col": pos - 1}, device_id_type=MESH,
        )

    def slopes_right(owner, k):
        return pltpu.make_async_remote_copy(
            src_ref=slopes.at[k, owner], dst_ref=slopes.at[k, owner],
            send_sem=spread_send.at[0, k, owner], recv_sem=spread_recv.at[0, k, owner],
            device_id={"col": pos + 1}, device_id_type=MESH,
        )

    def slopes_left(owner, k):
        return pltpu.make_async_remote_copy(
            src_ref=slopes.at[k, owner], dst_ref=slopes.at[k, owner],
            send_sem=spread_send.at[1, k, owner], recv_sem=spread_recv.at[1, k, owner],
            device_id={"col": pos - 1}, device_id_type=MESH,
        )

    def make_partials(k):
        mean = total[k] + dot(hub_in[...], hub_pick[:, cols(k, width)], 0, 0)
        mean = mean + dot(slot_in[...], recv_pick[cols(k, width), :], 1, 1)
        joined[k, narrow:, :] = (mean / degree[k, 0:1, :]).astype(BF16)
        partial[k] = dot(w_turned[...], joined[k], 1, 0).reshape(n, narrow, width)

    def sums_right(k):
        def step(s, carry):
            far = n - 1 - s

            @pl.when(jnp.logical_and(far > pos, has_left))
            def _():
                right_copy(far, k).wait_recv()
                to_right[k, far] = (partial[k, far] + from_left[k, far].astype(F32)).astype(BF16)

            @pl.when(jnp.logical_and(far > pos, jnp.logical_not(has_left)))
            def _():
                to_right[k, far] = partial[k, far].astype(BF16)

            @pl.when(far > pos)
            def _():
                right_copy(far, k).start()

            return carry

        lax.fori_loop(0, n - 1, step, 0)

    def sums_left(k):
        def step(s, carry):
            @pl.when(jnp.logical_and(s < pos, has_right))
            def _():
                left_copy(s, k).wait_recv()
                to_left[k, s] = (partial[k, s] + from_right[k, s].astype(F32)).astype(BF16)

            @pl.when(jnp.logical_and(s < pos, jnp.logical_not(has_right)))
            def _():
                to_left[k, s] = partial[k, s].astype(BF16)

            @pl.when(s < pos)
            def _():
                left_copy(s, k).start()

            return carry

        lax.fori_loop(0, n - 1, step, 0)

    def finish_preact(k):
        total[k] = partial[k, pos]

        @pl.when(has_left)
        def _():
            right_copy(pos, k).wait_recv()
            total[k] = total[k] + from_left[k, pos].astype(F32)

        @pl.when(has_right)
        def _():
            left_copy(pos, k).wait_recv()
            total[k] = total[k] + from_right[k, pos].astype(F32)

        preact = total[k]
        gate = jax.nn.sigmoid(preact)
        slope = gate * (1.0 + preact * (1.0 - gate))
        slopes[k, pos] = (cot[:, cols(k, width)].astype(F32) * slope).astype(BF16)

        @pl.when(has_right)
        def _():
            slopes_right(pos, k).start()

        @pl.when(has_left)
        def _():
            slopes_left(pos, k).start()

        hidden[:, cols(k, width)] = (preact * gate).astype(BF16)

    def turns_to_finish(owner):
        return jnp.maximum(owner, n - 1 - owner)

    def pass_on(d, t):
        def due(owner):
            k = t - turns_to_finish(owner) - d
            inside = jnp.logical_and(owner >= 0, owner < n)
            return k, jnp.logical_and(inside, jnp.logical_and(k >= 0, k < chunks))

        left_owner = pos - d
        k_left, due_left = due(left_owner)

        @pl.when(due_left)
        def _():
            slopes_right(left_owner, k_left).wait_recv()

            @pl.when(has_right)
            def _():
                slopes_right(left_owner, k_left).start()

        right_owner = pos + d
        k_right, due_right = due(right_owner)

        @pl.when(due_right)
        def _():
            slopes_left(right_owner, k_right).wait_recv()

            @pl.when(has_left)
            def _():
                slopes_left(right_owner, k_right).start()

    def backward(k):
        wide = jnp.concatenate(
            [slopes[k - 1].reshape(n * narrow, width), slopes[k].reshape(n * narrow, width)], axis=1
        )
        back = dot(w_neigh[...], wide, 1, 0)
        own = dot(w_self[...], wide, 1, 0)
        for half in range(2):
            at = k - 1 + half
            there = slice(half * width, (half + 1) * width)
            share[:, cols(at, width)] = (back[:, there] / degree[at, 0:1, :]).astype(BF16)
            direct[at] = own[:, there]
        weight_acc[...] += dot(jnp.concatenate([joined[k - 1], joined[k]], axis=1), wide, 1, 1)

    def when_inside(k, work):
        @pl.when(jnp.logical_and(k >= 0, k < chunks))
        def _():
            work(k)

    def turn(t, carry):
        def passing(d, inner):
            pass_on(d, t)
            return inner

        when_inside(t, make_partials)
        when_inside(t - pos, sums_right)
        when_inside(t - (n - 1 - pos), sums_left)
        when_inside(t - turns_to_finish(pos), finish_preact)

        @pl.when(t + 2 < chunks)
        def _():
            prepare(t + 2)

        lax.fori_loop(1, n, passing, 0)
        late = t - 2 * (n - 1)

        @pl.when(jnp.logical_and(late >= 0, lax.rem(late, 2) == 1))
        def _():
            backward(late)

        return carry

    lax.fori_loop(0, chunks + 2 * (n - 1), turn, 0)

    weight_out[...] = weight_acc[...].astype(BF16)
    for c in range(chips):
        twin_copy(c).start()
    def back_slots(i, carry):
        back_out[:, cols(i, tile)] = dot(share[...], recv_pick[:, cols(i, tile)], 1, 0).astype(BF16)
        return carry

    lax.fori_loop(0, peers * slots // tile, back_slots, 0)
    for d in range(1, peers):
        back_copy(d).start()
    hub_back_out[...] = dot(hub_pick[...], share[...], 1, 1)
    for d in range(1, peers):
        hub_back_copy(d).start()
    back_in[:, cols(me, slots)] = back_out[:, cols(me, slots)]
    hub_back_in[me] = hub_back_out[cols(me, hubs), :]
    for c in range(chips):
        twin_copy(c).wait_recv()
        rows, columns = part(2 * c + core)
        weight_half[c] = (weight_acc[rows, columns] + twin_in[c].astype(F32)).astype(BF16)
    for d in range(1, chips):
        weight_copy(d).start()

    def local_back(k, carry):
        direct[k] = direct[k] + dot(share[...], loc_pick[cols(k, width), :], 1, 1)
        return carry

    lax.fori_loop(0, chunks, local_back, 0)
    for d in range(1, peers):
        back_copy(d).wait_recv()
        hub_back_copy(d).wait_recv()
    hub_total = hub_back_in[0]
    for r in range(1, peers):
        hub_total = hub_total + hub_back_in[r]
    hub_total = hub_total.T
    hub_high = hub_total.astype(BF16)
    hub_low = (hub_total - hub_high.astype(F32)).astype(BF16)

    my_rows, my_cols = part(me)
    sums = weight_acc[my_rows, my_cols] + twin_in[chip].astype(F32)
    for d in range(1, chips):
        weight_copy(d).wait_recv()
        sums = sums + weight_in[lax.rem(chip + chips - d, chips)].astype(F32)
    weight_sum[...] = sums.astype(BF16)
    for d in range(1, chips):
        weight_share(d).start()
    weight_all[my_rows, my_cols] = weight_sum[...]
    weight_twin(0).start()

    def finish_grad(k, carry):
        grad = direct[k] + dot(back_in[...], send_pick[cols(k, width), :], 1, 1)
        grad = grad + dot(hub_high, own_pick[cols(k, width), :], 1, 1)
        grad = grad + dot(hub_low, own_pick[cols(k, width), :], 1, 1)
        grad_feats[:, cols(k, width)] = grad.astype(BF16)
        return carry

    lax.fori_loop(0, chunks, finish_grad, 0)
    def source_chip(d):
        return chips - d if d else 0

    for d in range(1, chips):
        weight_share(d).wait_recv()
        weight_twin(source_chip(d)).start()
    for d in range(chips):
        weight_twin_in(d).wait_recv()

    for d in range(1, peers):
        slot_copy(d).wait_send()
        hub_copy(d).wait_send()
        back_copy(d).wait_send()
        hub_back_copy(d).wait_send()
    for d in range(chips):
        twin_copy(d).wait_send()
        weight_twin(d).wait_send()
    for d in range(1, chips):
        weight_copy(d).wait_send()
        weight_share(d).wait_send()

    def drain(i, carry):
        k = lax.div(i, n)
        owner = lax.rem(i, n)

        @pl.when(owner > pos)
        def _():
            right_copy(owner, k).wait_send()

        @pl.when(owner < pos)
        def _():
            left_copy(owner, k).wait_send()

        @pl.when(jnp.logical_and(owner <= pos, has_right))
        def _():
            slopes_right(owner, k).wait_send()

        @pl.when(jnp.logical_and(owner >= pos, has_left))
        def _():
            slopes_left(owner, k).wait_send()

        return carry

    lax.fori_loop(0, chunks * n, drain, 0)


def per_device(n, peers, feats, w_self, w_neigh, cotangent, loc_nbr, send_rows, recv_node, hub_rows, hub_nbr):
    narrow, nodes = feats.shape
    chunks = 8
    width = nodes // chunks
    full = w_self.shape[1]
    hubs = hub_rows.shape[0]
    every = peers * send_rows.shape[2]
    lane_parts = min(peers, full // 128)
    piece = (2 * narrow * lane_parts // peers, full // lane_parts)
    vmem = pltpu.VMEM
    out = jax.ShapeDtypeStruct
    hidden, grad_feats, weight_all = pl.pallas_call(
        functools.partial(layer_kernel, n, peers, chunks),
        out_shape=(
            out((narrow, nodes), BF16), out((narrow, nodes), BF16),
            out((2 * narrow, full), BF16),
        ),
        in_specs=[pl.BlockSpec(memory_space=vmem)] * 9,
        out_specs=[pl.BlockSpec(memory_space=vmem)] * 3,
        scratch_shapes=[
            vmem((nodes, nodes), BF16), vmem((nodes, every), BF16), vmem((nodes, every), BF16),
            vmem((peers * hubs, nodes), BF16), vmem((nodes, hubs), BF16), vmem((chunks, 16, width), F32),
            vmem((narrow, every), BF16), vmem((narrow, every), BF16),
            vmem((hubs, narrow), BF16), vmem((peers * hubs, narrow), BF16),
            vmem((full, 2 * narrow), BF16), vmem((chunks, n, narrow, width), F32),
            vmem((chunks, narrow, width), F32), vmem((chunks, 2 * narrow, width), BF16),
            vmem((chunks, n, narrow, width), BF16), vmem((chunks, n, narrow, width), BF16),
            vmem((chunks, n, narrow, width), BF16), vmem((chunks, n, narrow, width), BF16),
            vmem((chunks, n, narrow, width), BF16),
            vmem((chunks, narrow, width), F32), vmem((narrow, nodes), BF16),
            vmem((2 * narrow, full), F32), vmem((2 * narrow, full), BF16), vmem((peers // 2,) + piece, BF16),
            vmem((peers // 2,) + piece, BF16), vmem((peers // 2,) + piece, BF16),
            vmem(piece, BF16),
            vmem((narrow, every), BF16), vmem((narrow, every), BF16),
            vmem((peers * hubs, narrow), F32), vmem((peers, hubs, narrow), F32),
            pltpu.SemaphoreType.DMA((8, peers)), pltpu.SemaphoreType.DMA((8, peers)),
            pltpu.SemaphoreType.DMA((2, chunks, n)), pltpu.SemaphoreType.DMA((2, chunks, n)),
            pltpu.SemaphoreType.DMA((2, chunks, n)), pltpu.SemaphoreType.DMA((2, chunks, n)),
        ],
        compiler_params=pltpu.CompilerParams(
            collective_id=0, has_side_effects=True, vmem_limit_bytes=60 * 1024 * 1024
        ),
    )(
        feats, w_self, w_neigh, cotangent, loc_nbr.T, send_rows.reshape(1, -1),
        recv_node.reshape(1, -1), hub_rows.reshape(1, -1), hub_nbr.T,
    )
    grads = weight_all.astype(F32)
    return hidden, grad_feats, grads[:narrow], grads[narrow:]


def solution(mesh):
    return jax.shard_map(
        functools.partial(per_device, mesh.shape["col"], mesh.shape["row"]),
        mesh=mesh,
        in_specs=(
            P("col", "row"),
            P("col", None),
            P("col", None),
            P("col", "row"),
            P("row", None),
            P("row", None, None),
            P("row", None, None),
            P("row"),
            P("row", None),
        ),
        out_specs=(P("col", "row"), P("col", "row"), P("col", None), P("col", None)),
        check_vma=False,
    )
```

```python
import functools

import jax
import jax.numpy as jnp
from jax import lax
from jax.experimental import pallas as pl
from jax.experimental.pallas import tpu as pltpu
from jax.sharding import PartitionSpec as P

BF16 = jnp.bfloat16
F32 = jnp.float32
MESH = pl.DeviceIdType.MESH


def dot(a, b, ca, cb):
    return lax.dot_general(a, b, (((ca,), (cb,)), ((), ())), preferred_element_type=F32)


def count_picks(indices, first, rows):
    names = lax.broadcasted_iota(jnp.int32, (rows, indices.shape[1]), 0) + first
    total = jnp.where(names == indices[0:1, :], 1.0, 0.0)
    for k in range(1, indices.shape[0]):
        total = total + jnp.where(names == indices[k : k + 1, :], 1.0, 0.0)
    return total.astype(BF16)


def fill_picks(dest, indices, strip):
    strip = min(strip, dest.shape[0])

    def body(i, carry):
        first = pl.multiple_of(i * strip, strip)
        dest[pl.ds(first, strip), :] = count_picks(indices, first, strip)
        return carry

    lax.fori_loop(0, dest.shape[0] // strip, body, 0)


def layer_kernel(
    n, peers, chunks,
    feats, w_self, w_neigh, cot, loc, send, recv, hub_row, hub,
    hidden, grad_feats, grad_self, grad_neigh,
    loc_pick, send_pick, recv_pick, hub_pick, own_pick, degree,
    slot_out, slot_in, hub_out, hub_in,
    w_turned, partial, total, joined, from_left, from_right, to_left, to_right, slopes,
    direct, share, weight_acc, weight_out, twin_in, weight_half, weight_in, weight_sum, weight_all,
    back_out, back_in, hub_back_out, hub_back_in,
    row_send, row_recv, sum_send, sum_recv, spread_send, spread_recv,
):
    narrow, nodes = feats.shape
    width = nodes // chunks
    slots = send.shape[1] // peers
    hubs = hub_row.shape[1]
    me = lax.axis_index("row")
    pos = lax.axis_index("col")
    has_left = pos > 0
    has_right = pos < n - 1

    def row_peer(d):
        return lax.rem(me + d, peers)

    def row_source(d):
        return lax.rem(me + peers - d, peers)

    barrier = pltpu.get_barrier_semaphore()
    for d in range(1, peers):
        pl.semaphore_signal(barrier, inc=1, device_id={"row": row_peer(d)}, device_id_type=MESH)

    @pl.when(has_left)
    def _():
        pl.semaphore_signal(barrier, inc=1, device_id={"col": pos - 1}, device_id_type=MESH)

    @pl.when(has_right)
    def _():
        pl.semaphore_signal(barrier, inc=1, device_id={"col": pos + 1}, device_id_type=MESH)

    def cols(index, size):
        return pl.ds(pl.multiple_of(index * size, size), size)

    def row_copy(src, dst, kind, d):
        return pltpu.make_async_remote_copy(
            src_ref=src, dst_ref=dst, send_sem=row_send.at[kind, d], recv_sem=row_recv.at[kind, d],
            device_id={"row": row_peer(d)}, device_id_type=MESH,
        )

    def slot_copy(d):
        return row_copy(slot_out.at[:, cols(row_peer(d), slots)], slot_in.at[:, cols(me, slots)], 0, d)

    def hub_copy(d):
        return row_copy(hub_out, hub_in.at[cols(me, hubs), :], 1, d)

    def back_copy(d):
        return row_copy(back_out.at[:, cols(row_peer(d), slots)], back_in.at[:, cols(me, slots)], 2, d)

    def hub_back_copy(d):
        return row_copy(hub_back_out.at[cols(row_peer(d), hubs), :], hub_back_in.at[me], 3, d)

    lane_parts = min(peers, weight_acc.shape[1] // 128)
    row_parts = peers // lane_parts
    part_rows = weight_acc.shape[0] // row_parts
    part_cols = weight_acc.shape[1] // lane_parts

    def part(r):
        return cols(lax.div(r, lane_parts), part_rows), cols(lax.rem(r, lane_parts), part_cols)

    chips = peers // 2
    chip = lax.div(me, 2)
    core = lax.rem(me, 2)
    twin = me + 1 - 2 * core

    def other_chip(d):
        return lax.rem(chip + d, chips)

    def to_row(src, dst, kind, index, peer):
        return pltpu.make_async_remote_copy(
            src_ref=src, dst_ref=dst, send_sem=row_send.at[kind, index], recv_sem=row_recv.at[kind, index],
            device_id={"row": peer}, device_id_type=MESH,
        )

    def twin_copy(c):
        rows, columns = part(2 * c + 1 - core)
        return to_row(weight_out.at[rows, columns], twin_in.at[c], 4, c, twin)

    def weight_copy(d):
        c = other_chip(d)
        return to_row(weight_half.at[c], weight_in.at[chip], 5, d, 2 * c + core)

    def weight_share(d):
        rows, columns = part(me)
        return to_row(weight_sum, weight_all.at[rows, columns], 6, d, 2 * other_chip(d) + core)

    def weight_twin(d):
        rows, columns = part(2 * other_chip(d) + core)
        return to_row(weight_all.at[rows, columns], weight_all.at[rows, columns], 7, d, twin)

    def weight_twin_in(d):
        rows, columns = part(2 * other_chip(d) + 1 - core)
        return to_row(weight_all.at[rows, columns], weight_all.at[rows, columns], 7, d, twin)

    fill_picks(own_pick, hub_row[...], 64)
    hub_out[...] = dot(feats[...], own_pick[...], 1, 0).T.astype(BF16)

    def gather_for(peer):
        here = cols(peer, slots)
        names = send[:, here]

        def rows(i, carry):
            first = pl.multiple_of(i * 128, 128)
            send_pick[pl.ds(first, 128), here] = count_picks(names, first, 128)
            return carry

        lax.fori_loop(0, nodes // 128, rows, 0)
        return dot(feats[...], send_pick[:, here], 1, 0).astype(BF16)

    pl.semaphore_wait(barrier, peers - 1 + has_left.astype(jnp.int32) + has_right.astype(jnp.int32))

    def gather_and_send(d, carry):
        slot_out[:, cols(row_peer(d), slots)] = gather_for(row_peer(d))
        slot_copy(d).start()
        hub_copy(d).start()
        return carry

    lax.fori_loop(1, peers, gather_and_send, 0)
    slot_in[:, cols(me, slots)] = gather_for(me)
    hub_in[cols(me, hubs), :] = hub_out[...]

    fixed = loc.shape[0] + hub.shape[0]

    def prepare(k):
        here = cols(k, width)
        names = loc[:, here]

        def local_rows(i, carry):
            first = pl.multiple_of(i * 128, 128)
            loc_pick[pl.ds(first, 128), here] = count_picks(names, first, 128)
            return carry

        lax.fori_loop(0, nodes // 128, local_rows, 0)
        targets = recv[...]

        def target_rows(i, carry):
            first = pl.multiple_of(k * width + i * 16, 16)
            recv_pick[pl.ds(first, 16), :] = count_picks(targets, first, 16)
            return carry

        lax.fori_loop(0, width // 16, target_rows, 0)
        hub_pick[:, here] = count_picks(hub[:, here], 0, hub_pick.shape[0])
        total[k] = dot(feats[...], loc_pick[:, here], 1, 0)
        ones = jnp.ones((16, recv_pick.shape[1]), BF16)
        degree[k] = dot(ones, recv_pick[here, :], 1, 1) + fixed
        joined[k, 0:narrow, :] = feats[:, here]

    prepare(0)
    prepare(1)
    w_turned[:, 0:narrow] = w_self[...].T
    w_turned[:, narrow:] = w_neigh[...].T
    weight_acc[...] = jnp.zeros_like(weight_acc)
    for d in range(1, peers):
        slot_copy(d).wait_recv()
        hub_copy(d).wait_recv()

    def right_copy(owner, k):
        return pltpu.make_async_remote_copy(
            src_ref=to_right.at[k, owner], dst_ref=from_left.at[k, owner],
            send_sem=sum_send.at[0, k, owner], recv_sem=sum_recv.at[0, k, owner],
            device_id={"col": pos + 1}, device_id_type=MESH,
        )

    def left_copy(owner, k):
        return pltpu.make_async_remote_copy(
            src_ref=to_left.at[k, owner], dst_ref=from_right.at[k, owner],
            send_sem=sum_send.at[1, k, owner], recv_sem=sum_recv.at[1, k, owner],
            device_id={"col": pos - 1}, device_id_type=MESH,
        )

    def slopes_right(owner, k):
        return pltpu.make_async_remote_copy(
            src_ref=slopes.at[k, owner], dst_ref=slopes.at[k, owner],
            send_sem=spread_send.at[0, k, owner], recv_sem=spread_recv.at[0, k, owner],
            device_id={"col": pos + 1}, device_id_type=MESH,
        )

    def slopes_left(owner, k):
        return pltpu.make_async_remote_copy(
            src_ref=slopes.at[k, owner], dst_ref=slopes.at[k, owner],
            send_sem=spread_send.at[1, k, owner], recv_sem=spread_recv.at[1, k, owner],
            device_id={"col": pos - 1}, device_id_type=MESH,
        )

    def make_partials(k):
        mean = total[k] + dot(hub_in[...], hub_pick[:, cols(k, width)], 0, 0)
        mean = mean + dot(slot_in[...], recv_pick[cols(k, width), :], 1, 1)
        joined[k, narrow:, :] = (mean / degree[k, 0:1, :]).astype(BF16)
        partial[k] = dot(w_turned[...], joined[k], 1, 0).reshape(n, narrow, width)

    def sums_right(k):
        def step(s, carry):
            far = n - 1 - s

            @pl.when(jnp.logical_and(far > pos, has_left))
            def _():
                right_copy(far, k).wait_recv()
                to_right[k, far] = (partial[k, far] + from_left[k, far].astype(F32)).astype(BF16)

            @pl.when(jnp.logical_and(far > pos, jnp.logical_not(has_left)))
            def _():
                to_right[k, far] = partial[k, far].astype(BF16)

            @pl.when(far > pos)
            def _():
                right_copy(far, k).start()

            return carry

        lax.fori_loop(0, n - 1, step, 0)

    def sums_left(k):
        def step(s, carry):
            @pl.when(jnp.logical_and(s < pos, has_right))
            def _():
                left_copy(s, k).wait_recv()
                to_left[k, s] = (partial[k, s] + from_right[k, s].astype(F32)).astype(BF16)

            @pl.when(jnp.logical_and(s < pos, jnp.logical_not(has_right)))
            def _():
                to_left[k, s] = partial[k, s].astype(BF16)

            @pl.when(s < pos)
            def _():
                left_copy(s, k).start()

            return carry

        lax.fori_loop(0, n - 1, step, 0)

    def finish_preact(k):
        total[k] = partial[k, pos]

        @pl.when(has_left)
        def _():
            right_copy(pos, k).wait_recv()
            total[k] = total[k] + from_left[k, pos].astype(F32)

        @pl.when(has_right)
        def _():
            left_copy(pos, k).wait_recv()
            total[k] = total[k] + from_right[k, pos].astype(F32)

        preact = total[k]
        gate = jax.nn.sigmoid(preact)
        slope = gate * (1.0 + preact * (1.0 - gate))
        slopes[k, pos] = (cot[:, cols(k, width)].astype(F32) * slope).astype(BF16)

        @pl.when(has_right)
        def _():
            slopes_right(pos, k).start()

        @pl.when(has_left)
        def _():
            slopes_left(pos, k).start()

        hidden[:, cols(k, width)] = (preact * gate).astype(BF16)

    def turns_to_finish(owner):
        return jnp.maximum(owner, n - 1 - owner)

    def pass_on(d, t):
        def due(owner):
            k = t - turns_to_finish(owner) - d
            inside = jnp.logical_and(owner >= 0, owner < n)
            return k, jnp.logical_and(inside, jnp.logical_and(k >= 0, k < chunks))

        left_owner = pos - d
        k_left, due_left = due(left_owner)

        @pl.when(due_left)
        def _():
            slopes_right(left_owner, k_left).wait_recv()

            @pl.when(has_right)
            def _():
                slopes_right(left_owner, k_left).start()

        right_owner = pos + d
        k_right, due_right = due(right_owner)

        @pl.when(due_right)
        def _():
            slopes_left(right_owner, k_right).wait_recv()

            @pl.when(has_left)
            def _():
                slopes_left(right_owner, k_right).start()

    def backward(k):
        wide = jnp.concatenate(
            [slopes[k - 1].reshape(n * narrow, width), slopes[k].reshape(n * narrow, width)], axis=1
        )
        back = dot(w_neigh[...], wide, 1, 0)
        own = dot(w_self[...], wide, 1, 0)
        for half in range(2):
            at = k - 1 + half
            there = slice(half * width, (half + 1) * width)
            share[:, cols(at, width)] = (back[:, there] / degree[at, 0:1, :]).astype(BF16)
            direct[at] = own[:, there]
        weight_acc[...] += dot(jnp.concatenate([joined[k - 1], joined[k]], axis=1), wide, 1, 1)

    def when_inside(k, work):
        @pl.when(jnp.logical_and(k >= 0, k < chunks))
        def _():
            work(k)

    def turn(t, carry):
        def passing(d, inner):
            pass_on(d, t)
            return inner

        when_inside(t, make_partials)
        when_inside(t - pos, sums_right)
        when_inside(t - (n - 1 - pos), sums_left)
        when_inside(t - turns_to_finish(pos), finish_preact)

        @pl.when(t + 2 < chunks)
        def _():
            prepare(t + 2)

        lax.fori_loop(1, n, passing, 0)
        late = t - 2 * (n - 1)

        @pl.when(jnp.logical_and(late >= 0, lax.rem(late, 2) == 1))
        def _():
            backward(late)

        return carry

    lax.fori_loop(0, chunks + 2 * (n - 1), turn, 0)

    weight_out[...] = weight_acc[...].astype(BF16)
    for c in range(chips):
        twin_copy(c).start()
    def back_slots(peer):
        return dot(share[...], recv_pick[:, cols(peer, slots)], 1, 0).astype(BF16)

    def back_and_send(d, carry):
        back_out[:, cols(row_peer(d), slots)] = back_slots(row_peer(d))
        back_copy(d).start()
        return carry

    lax.fori_loop(1, peers, back_and_send, 0)
    hub_back_out[...] = dot(hub_pick[...], share[...], 1, 1)
    for d in range(1, peers):
        hub_back_copy(d).start()
    back_in[:, cols(me, slots)] = back_slots(me)
    hub_back_in[me] = hub_back_out[cols(me, hubs), :]
    for d in range(1, chips):
        c = other_chip(d)
        twin_copy(c).wait_recv()
        rows, columns = part(2 * c + core)
        weight_half[c] = (weight_acc[rows, columns] + twin_in[c].astype(F32)).astype(BF16)
        weight_copy(d).start()
    twin_copy(chip).wait_recv()

    def local_back(k, carry):
        direct[k] = direct[k] + dot(share[...], loc_pick[cols(k, width), :], 1, 1)
        return carry

    lax.fori_loop(0, chunks, local_back, 0)
    for d in range(1, peers):
        back_copy(d).wait_recv()
        hub_back_copy(d).wait_recv()
    hub_total = hub_back_in[0]
    for r in range(1, peers):
        hub_total = hub_total + hub_back_in[r]
    hub_total = hub_total.T
    hub_high = hub_total.astype(BF16)
    hub_low = (hub_total - hub_high.astype(F32)).astype(BF16)

    my_rows, my_cols = part(me)
    sums = weight_acc[my_rows, my_cols] + twin_in[chip].astype(F32)
    for d in range(1, chips):
        weight_copy(d).wait_recv()
        sums = sums + weight_in[lax.rem(chip + chips - d, chips)].astype(F32)
    weight_sum[...] = sums.astype(BF16)
    for d in range(1, chips):
        weight_share(d).start()
    weight_all[my_rows, my_cols] = weight_sum[...]
    weight_twin(0).start()

    def finish_grad(k, carry):
        grad = direct[k] + dot(back_in[...], send_pick[cols(k, width), :], 1, 1)
        grad = grad + dot(hub_high, own_pick[cols(k, width), :], 1, 1)
        grad = grad + dot(hub_low, own_pick[cols(k, width), :], 1, 1)
        grad_feats[:, cols(k, width)] = grad.astype(BF16)
        return carry

    lax.fori_loop(0, chunks, finish_grad, 0)
    def source_chip(d):
        return chips - d if d else 0

    for d in range(1, chips):
        weight_share(d).wait_recv()
        weight_twin(source_chip(d)).start()
    for d in range(chips):
        weight_twin_in(d).wait_recv()
    grad_self[...] = weight_all[0:narrow, :]
    grad_neigh[...] = weight_all[narrow:, :]

    for d in range(1, peers):
        slot_copy(d).wait_send()
        hub_copy(d).wait_send()
        back_copy(d).wait_send()
        hub_back_copy(d).wait_send()
    for d in range(chips):
        twin_copy(d).wait_send()
        weight_twin(d).wait_send()
    for d in range(1, chips):
        weight_copy(d).wait_send()
        weight_share(d).wait_send()

    def drain(i, carry):
        k = lax.div(i, n)
        owner = lax.rem(i, n)

        @pl.when(owner > pos)
        def _():
            right_copy(owner, k).wait_send()

        @pl.when(owner < pos)
        def _():
            left_copy(owner, k).wait_send()

        @pl.when(jnp.logical_and(owner <= pos, has_right))
        def _():
            slopes_right(owner, k).wait_send()

        @pl.when(jnp.logical_and(owner >= pos, has_left))
        def _():
            slopes_left(owner, k).wait_send()

        return carry

    lax.fori_loop(0, chunks * n, drain, 0)


def per_device(n, peers, feats, w_self, w_neigh, cotangent, loc_nbr, send_rows, recv_node, hub_rows, hub_nbr):
    narrow, nodes = feats.shape
    chunks = 8
    width = nodes // chunks
    full = w_self.shape[1]
    hubs = hub_rows.shape[0]
    every = peers * send_rows.shape[2]
    lane_parts = min(peers, full // 128)
    piece = (2 * narrow * lane_parts // peers, full // lane_parts)
    vmem = pltpu.VMEM
    out = jax.ShapeDtypeStruct
    hidden, grad_feats, grad_self, grad_neigh = pl.pallas_call(
        functools.partial(layer_kernel, n, peers, chunks),
        out_shape=(
            out((narrow, nodes), BF16), out((narrow, nodes), BF16),
            out((narrow, full), BF16), out((narrow, full), BF16),
        ),
        in_specs=[pl.BlockSpec(memory_space=vmem)] * 9,
        out_specs=[pl.BlockSpec(memory_space=vmem)] * 4,
        scratch_shapes=[
            vmem((nodes, nodes), BF16), vmem((nodes, every), BF16), vmem((nodes, every), BF16),
            vmem((peers * hubs, nodes), BF16), vmem((nodes, hubs), BF16), vmem((chunks, 16, width), F32),
            vmem((narrow, every), BF16), vmem((narrow, every), BF16),
            vmem((hubs, narrow), BF16), vmem((peers * hubs, narrow), BF16),
            vmem((full, 2 * narrow), BF16), vmem((chunks, n, narrow, width), F32),
            vmem((chunks, narrow, width), F32), vmem((chunks, 2 * narrow, width), BF16),
            vmem((chunks, n, narrow, width), BF16), vmem((chunks, n, narrow, width), BF16),
            vmem((chunks, n, narrow, width), BF16), vmem((chunks, n, narrow, width), BF16),
            vmem((chunks, n, narrow, width), BF16),
            vmem((chunks, narrow, width), F32), vmem((narrow, nodes), BF16),
            vmem((2 * narrow, full), F32), vmem((2 * narrow, full), BF16), vmem((peers // 2,) + piece, BF16),
            vmem((peers // 2,) + piece, BF16), vmem((peers // 2,) + piece, BF16),
            vmem(piece, BF16), vmem((2 * narrow, full), BF16),
            vmem((narrow, every), BF16), vmem((narrow, every), BF16),
            vmem((peers * hubs, narrow), F32), vmem((peers, hubs, narrow), F32),
            pltpu.SemaphoreType.DMA((8, peers)), pltpu.SemaphoreType.DMA((8, peers)),
            pltpu.SemaphoreType.DMA((2, chunks, n)), pltpu.SemaphoreType.DMA((2, chunks, n)),
            pltpu.SemaphoreType.DMA((2, chunks, n)), pltpu.SemaphoreType.DMA((2, chunks, n)),
        ],
        compiler_params=pltpu.CompilerParams(
            collective_id=0, has_side_effects=True, vmem_limit_bytes=60 * 1024 * 1024
        ),
    )(
        feats, w_self, w_neigh, cotangent, loc_nbr.T, send_rows.reshape(1, -1),
        recv_node.reshape(1, -1), hub_rows.reshape(1, -1), hub_nbr.T,
    )
    return hidden, grad_feats, grad_self.astype(F32), grad_neigh.astype(F32)


def solution(mesh):
    return jax.shard_map(
        functools.partial(per_device, mesh.shape["col"], mesh.shape["row"]),
        mesh=mesh,
        in_specs=(
            P("col", "row"),
            P("col", None),
            P("col", None),
            P("col", "row"),
            P("row", None),
            P("row", None, None),
            P("row", None, None),
            P("row"),
            P("row", None),
        ),
        out_specs=(P("col", "row"), P("col", "row"), P("col", None), P("col", None)),
        check_vma=False,
    )
```

```python
import functools

import jax
import jax.numpy as jnp
from jax import lax
from jax.experimental import pallas as pl
from jax.experimental.pallas import tpu as pltpu
from jax.sharding import PartitionSpec as P

BF16 = jnp.bfloat16
F32 = jnp.float32
MESH = pl.DeviceIdType.MESH


def dot(a, b, ca, cb):
    return lax.dot_general(a, b, (((ca,), (cb,)), ((), ())), preferred_element_type=F32)


def count_picks(indices, first, rows):
    names = lax.broadcasted_iota(jnp.int32, (rows, indices.shape[1]), 0) + first
    total = jnp.where(names == indices[0:1, :], 1.0, 0.0)
    for k in range(1, indices.shape[0]):
        total = total + jnp.where(names == indices[k : k + 1, :], 1.0, 0.0)
    return total.astype(BF16)


def fill_picks(dest, indices, strip):
    strip = min(strip, dest.shape[0])

    def body(i, carry):
        first = pl.multiple_of(i * strip, strip)
        dest[pl.ds(first, strip), :] = count_picks(indices, first, strip)
        return carry

    lax.fori_loop(0, dest.shape[0] // strip, body, 0)


def layer_kernel(
    n, peers, chunks,
    feats, w_self, w_neigh, cot, loc, send, recv, hub_row, hub,
    hidden, grad_feats, weight_all,
    loc_pick, send_pick, recv_pick, hub_pick, own_pick, degree,
    slot_out, slot_in, hub_out, hub_in,
    w_turned, partial, total, joined, from_left, from_right, to_left, to_right, slopes,
    direct, share, weight_acc, weight_out, twin_in, weight_half, weight_in, weight_sum,
    back_out, back_in, hub_back_out, hub_back_in,
    row_send, row_recv, sum_send, sum_recv, spread_send, spread_recv,
):
    narrow, nodes = feats.shape
    width = nodes // chunks
    slots = send.shape[1] // peers
    hubs = hub_row.shape[1]
    me = lax.axis_index("row")
    pos = lax.axis_index("col")
    has_left = pos > 0
    has_right = pos < n - 1

    def row_peer(d):
        return lax.rem(me + d, peers)

    def row_source(d):
        return lax.rem(me + peers - d, peers)

    barrier = pltpu.get_barrier_semaphore()
    for d in range(1, peers):
        pl.semaphore_signal(barrier, inc=1, device_id={"row": row_peer(d)}, device_id_type=MESH)

    @pl.when(has_left)
    def _():
        pl.semaphore_signal(barrier, inc=1, device_id={"col": pos - 1}, device_id_type=MESH)

    @pl.when(has_right)
    def _():
        pl.semaphore_signal(barrier, inc=1, device_id={"col": pos + 1}, device_id_type=MESH)

    def cols(index, size):
        return pl.ds(pl.multiple_of(index * size, size), size)

    def row_copy(src, dst, kind, d):
        return pltpu.make_async_remote_copy(
            src_ref=src, dst_ref=dst, send_sem=row_send.at[kind, d], recv_sem=row_recv.at[kind, d],
            device_id={"row": row_peer(d)}, device_id_type=MESH,
        )

    def slot_copy(d):
        return row_copy(slot_out.at[:, cols(row_peer(d), slots)], slot_in.at[:, cols(me, slots)], 0, d)

    def hub_copy(d):
        return row_copy(hub_out, hub_in.at[cols(me, hubs), :], 1, d)

    def back_copy(d):
        return row_copy(back_out.at[:, cols(row_peer(d), slots)], back_in.at[:, cols(me, slots)], 2, d)

    def hub_back_copy(d):
        return row_copy(hub_back_out.at[cols(row_peer(d), hubs), :], hub_back_in.at[me], 3, d)

    lane_parts = min(peers, weight_acc.shape[1] // 128)
    row_parts = peers // lane_parts
    part_rows = weight_acc.shape[0] // row_parts
    part_cols = weight_acc.shape[1] // lane_parts

    def part(r):
        return cols(lax.div(r, lane_parts), part_rows), cols(lax.rem(r, lane_parts), part_cols)

    chips = peers // 2
    chip = lax.div(me, 2)
    core = lax.rem(me, 2)
    twin = me + 1 - 2 * core

    def other_chip(d):
        return lax.rem(chip + d, chips)

    def to_row(src, dst, kind, index, peer):
        return pltpu.make_async_remote_copy(
            src_ref=src, dst_ref=dst, send_sem=row_send.at[kind, index], recv_sem=row_recv.at[kind, index],
            device_id={"row": peer}, device_id_type=MESH,
        )

    def twin_copy(c):
        rows, columns = part(2 * c + 1 - core)
        return to_row(weight_out.at[rows, columns], twin_in.at[c], 4, c, twin)

    def weight_copy(d):
        c = other_chip(d)
        return to_row(weight_half.at[c], weight_in.at[chip], 5, d, 2 * c + core)

    def weight_share(d):
        rows, columns = part(me)
        return to_row(weight_sum, weight_all.at[rows, columns], 6, d, 2 * other_chip(d) + core)

    def weight_twin(d):
        rows, columns = part(2 * other_chip(d) + core)
        return to_row(weight_all.at[rows, columns], weight_all.at[rows, columns], 7, d, twin)

    def weight_twin_in(d):
        rows, columns = part(2 * other_chip(d) + 1 - core)
        return to_row(weight_all.at[rows, columns], weight_all.at[rows, columns], 7, d, twin)

    fill_picks(send_pick, send[...], 16)
    fill_picks(own_pick, hub_row[...], 64)
    hub_out[...] = dot(feats[...], own_pick[...], 1, 0).T.astype(BF16)

    tile = 2 * slots

    def gather_out(i, carry):
        slot_out[:, cols(i, tile)] = dot(feats[...], send_pick[:, cols(i, tile)], 1, 0).astype(BF16)
        return carry

    lax.fori_loop(0, peers * slots // tile, gather_out, 0)

    pl.semaphore_wait(barrier, peers - 1 + has_left.astype(jnp.int32) + has_right.astype(jnp.int32))
    for d in range(1, peers):
        slot_copy(d).start()
        hub_copy(d).start()
    slot_in[:, cols(me, slots)] = slot_out[:, cols(me, slots)]
    hub_in[cols(me, hubs), :] = hub_out[...]

    fixed = loc.shape[0] + hub.shape[0]

    def prepare(k):
        here = cols(k, width)
        names = loc[:, here]

        def local_rows(i, carry):
            first = pl.multiple_of(i * 128, 128)
            loc_pick[pl.ds(first, 128), here] = count_picks(names, first, 128)
            return carry

        lax.fori_loop(0, nodes // 128, local_rows, 0)
        targets = recv[...]

        def target_rows(i, carry):
            first = pl.multiple_of(k * width + i * 16, 16)
            recv_pick[pl.ds(first, 16), :] = count_picks(targets, first, 16)
            return carry

        lax.fori_loop(0, width // 16, target_rows, 0)
        hub_pick[:, here] = count_picks(hub[:, here], 0, hub_pick.shape[0])
        total[k] = dot(feats[...], loc_pick[:, here], 1, 0)
        ones = jnp.ones((16, recv_pick.shape[1]), BF16)
        degree[k] = dot(ones, recv_pick[here, :], 1, 1) + fixed
        joined[k, 0:narrow, :] = feats[:, here]

    prepare(0)
    w_turned[:, 0:narrow] = w_self[...].T
    w_turned[:, narrow:] = w_neigh[...].T
    weight_acc[...] = jnp.zeros_like(weight_acc)
    for d in range(1, peers):
        slot_copy(d).wait_recv()
        hub_copy(d).wait_recv()

    def right_copy(owner, k):
        return pltpu.make_async_remote_copy(
            src_ref=to_right.at[k, owner], dst_ref=from_left.at[k, owner],
            send_sem=sum_send.at[0, k, owner], recv_sem=sum_recv.at[0, k, owner],
            device_id={"col": pos + 1}, device_id_type=MESH,
        )

    def left_copy(owner, k):
        return pltpu.make_async_remote_copy(
            src_ref=to_left.at[k, owner], dst_ref=from_right.at[k, owner],
            send_sem=sum_send.at[1, k, owner], recv_sem=sum_recv.at[1, k, owner],
            device_id={"col": pos - 1}, device_id_type=MESH,
        )

    def slopes_right(owner, k):
        return pltpu.make_async_remote_copy(
            src_ref=slopes.at[k, owner], dst_ref=slopes.at[k, owner],
            send_sem=spread_send.at[0, k, owner], recv_sem=spread_recv.at[0, k, owner],
            device_id={"col": pos + 1}, device_id_type=MESH,
        )

    def slopes_left(owner, k):
        return pltpu.make_async_remote_copy(
            src_ref=slopes.at[k, owner], dst_ref=slopes.at[k, owner],
            send_sem=spread_send.at[1, k, owner], recv_sem=spread_recv.at[1, k, owner],
            device_id={"col": pos - 1}, device_id_type=MESH,
        )

    def make_partials(k):
        mean = total[k] + dot(hub_in[...], hub_pick[:, cols(k, width)], 0, 0)
        mean = mean + dot(slot_in[...], recv_pick[cols(k, width), :], 1, 1)
        joined[k, narrow:, :] = (mean / degree[k, 0:1, :]).astype(BF16)
        partial[k] = dot(w_turned[...], joined[k], 1, 0).reshape(n, narrow, width)

    def sums_right(k):
        def step(s, carry):
            far = n - 1 - s

            @pl.when(jnp.logical_and(far > pos, has_left))
            def _():
                right_copy(far, k).wait_recv()
                to_right[k, far] = (partial[k, far] + from_left[k, far].astype(F32)).astype(BF16)

            @pl.when(jnp.logical_and(far > pos, jnp.logical_not(has_left)))
            def _():
                to_right[k, far] = partial[k, far].astype(BF16)

            @pl.when(far > pos)
            def _():
                right_copy(far, k).start()

            return carry

        lax.fori_loop(0, n - 1, step, 0)

    def sums_left(k):
        def step(s, carry):
            @pl.when(jnp.logical_and(s < pos, has_right))
            def _():
                left_copy(s, k).wait_recv()
                to_left[k, s] = (partial[k, s] + from_right[k, s].astype(F32)).astype(BF16)

            @pl.when(jnp.logical_and(s < pos, jnp.logical_not(has_right)))
            def _():
                to_left[k, s] = partial[k, s].astype(BF16)

            @pl.when(s < pos)
            def _():
                left_copy(s, k).start()

            return carry

        lax.fori_loop(0, n - 1, step, 0)

    def finish_preact(k):
        total[k] = partial[k, pos]

        @pl.when(has_left)
        def _():
            right_copy(pos, k).wait_recv()
            total[k] = total[k] + from_left[k, pos].astype(F32)

        @pl.when(has_right)
        def _():
            left_copy(pos, k).wait_recv()
            total[k] = total[k] + from_right[k, pos].astype(F32)

        preact = total[k]
        gate = jax.nn.sigmoid(preact)
        slope = gate * (1.0 + preact * (1.0 - gate))
        slopes[k, pos] = (cot[:, cols(k, width)].astype(F32) * slope).astype(BF16)

        @pl.when(has_right)
        def _():
            slopes_right(pos, k).start()

        @pl.when(has_left)
        def _():
            slopes_left(pos, k).start()

        hidden[:, cols(k, width)] = (preact * gate).astype(BF16)

    def turns_to_finish(owner):
        return jnp.maximum(owner, n - 1 - owner)

    def pass_on(d, t):
        def due(owner):
            k = t - turns_to_finish(owner) - d
            inside = jnp.logical_and(owner >= 0, owner < n)
            return k, jnp.logical_and(inside, jnp.logical_and(k >= 0, k < chunks))

        left_owner = pos - d
        k_left, due_left = due(left_owner)

        @pl.when(due_left)
        def _():
            slopes_right(left_owner, k_left).wait_recv()

            @pl.when(has_right)
            def _():
                slopes_right(left_owner, k_left).start()

        right_owner = pos + d
        k_right, due_right = due(right_owner)

        @pl.when(due_right)
        def _():
            slopes_left(right_owner, k_right).wait_recv()

            @pl.when(has_left)
            def _():
                slopes_left(right_owner, k_right).start()

    def backward(k):
        wide = jnp.concatenate(
            [slopes[k - 1].reshape(n * narrow, width), slopes[k].reshape(n * narrow, width)], axis=1
        )
        back = dot(w_neigh[...], wide, 1, 0)
        own = dot(w_self[...], wide, 1, 0)
        for half in range(2):
            at = k - 1 + half
            there = slice(half * width, (half + 1) * width)
            share[:, cols(at, width)] = (back[:, there] / degree[at, 0:1, :]).astype(BF16)
            direct[at] = own[:, there]
        weight_acc[...] += dot(jnp.concatenate([joined[k - 1], joined[k]], axis=1), wide, 1, 1)

    def when_inside(k, work):
        @pl.when(jnp.logical_and(k >= 0, k < chunks))
        def _():
            work(k)

    def turn(t, carry):
        def passing(d, inner):
            pass_on(d, t)
            return inner

        when_inside(t, make_partials)
        when_inside(t - pos, sums_right)
        when_inside(t - (n - 1 - pos), sums_left)
        when_inside(t - turns_to_finish(pos), finish_preact)

        @pl.when(t + 1 < chunks)
        def _():
            prepare(t + 1)

        lax.fori_loop(1, n, passing, 0)
        late = t - 2 * (n - 1)

        @pl.when(jnp.logical_and(late >= 0, lax.rem(late, 2) == 1))
        def _():
            backward(late)

        return carry

    lax.fori_loop(0, chunks + 2 * (n - 1), turn, 0)

    weight_out[...] = weight_acc[...].astype(BF16)
    for c in range(chips):
        twin_copy(c).start()
    def back_slots(i, carry):
        back_out[:, cols(i, tile)] = dot(share[...], recv_pick[:, cols(i, tile)], 1, 0).astype(BF16)
        return carry

    lax.fori_loop(0, peers * slots // tile, back_slots, 0)
    for d in range(1, peers):
        back_copy(d).start()
    hub_back_out[...] = dot(hub_pick[...], share[...], 1, 1)
    for d in range(1, peers):
        hub_back_copy(d).start()
    back_in[:, cols(me, slots)] = back_out[:, cols(me, slots)]
    hub_back_in[me] = hub_back_out[cols(me, hubs), :]
    for d in range(1, chips):
        c = other_chip(d)
        twin_copy(c).wait_recv()
        rows, columns = part(2 * c + core)
        weight_half[c] = (weight_acc[rows, columns] + twin_in[c].astype(F32)).astype(BF16)
        weight_copy(d).start()
    twin_copy(chip).wait_recv()

    def local_back(k, carry):
        direct[k] = direct[k] + dot(share[...], loc_pick[cols(k, width), :], 1, 1)
        return carry

    lax.fori_loop(0, chunks, local_back, 0)
    for d in range(1, peers):
        back_copy(d).wait_recv()
        hub_back_copy(d).wait_recv()
    hub_total = hub_back_in[0]
    for r in range(1, peers):
        hub_total = hub_total + hub_back_in[r]
    hub_total = hub_total.T
    hub_high = hub_total.astype(BF16)
    hub_low = (hub_total - hub_high.astype(F32)).astype(BF16)

    my_rows, my_cols = part(me)
    sums = weight_acc[my_rows, my_cols] + twin_in[chip].astype(F32)
    for d in range(1, chips):
        weight_copy(d).wait_recv()
        sums = sums + weight_in[lax.rem(chip + chips - d, chips)].astype(F32)
    weight_sum[...] = sums.astype(BF16)
    for d in range(1, chips):
        weight_share(d).start()
    weight_all[my_rows, my_cols] = weight_sum[...]
    weight_twin(0).start()

    def finish_grad(k, carry):
        grad = direct[k] + dot(back_in[...], send_pick[cols(k, width), :], 1, 1)
        grad = grad + dot(hub_high, own_pick[cols(k, width), :], 1, 1)
        grad = grad + dot(hub_low, own_pick[cols(k, width), :], 1, 1)
        grad_feats[:, cols(k, width)] = grad.astype(BF16)
        return carry

    lax.fori_loop(0, chunks, finish_grad, 0)
    def source_chip(d):
        return chips - d if d else 0

    for d in range(1, chips):
        weight_share(d).wait_recv()
        weight_twin(source_chip(d)).start()
    for d in range(chips):
        weight_twin_in(d).wait_recv()

    for d in range(1, peers):
        slot_copy(d).wait_send()
        hub_copy(d).wait_send()
        back_copy(d).wait_send()
        hub_back_copy(d).wait_send()
    for d in range(chips):
        twin_copy(d).wait_send()
        weight_twin(d).wait_send()
    for d in range(1, chips):
        weight_copy(d).wait_send()
        weight_share(d).wait_send()

    def drain(i, carry):
        k = lax.div(i, n)
        owner = lax.rem(i, n)

        @pl.when(owner > pos)
        def _():
            right_copy(owner, k).wait_send()

        @pl.when(owner < pos)
        def _():
            left_copy(owner, k).wait_send()

        @pl.when(jnp.logical_and(owner <= pos, has_right))
        def _():
            slopes_right(owner, k).wait_send()

        @pl.when(jnp.logical_and(owner >= pos, has_left))
        def _():
            slopes_left(owner, k).wait_send()

        return carry

    lax.fori_loop(0, chunks * n, drain, 0)


def per_device(n, peers, feats, w_self, w_neigh, cotangent, loc_nbr, send_rows, recv_node, hub_rows, hub_nbr):
    narrow, nodes = feats.shape
    chunks = 8
    width = nodes // chunks
    full = w_self.shape[1]
    hubs = hub_rows.shape[0]
    every = peers * send_rows.shape[2]
    lane_parts = min(peers, full // 128)
    piece = (2 * narrow * lane_parts // peers, full // lane_parts)
    vmem = pltpu.VMEM
    out = jax.ShapeDtypeStruct
    hidden, grad_feats, weight_all = pl.pallas_call(
        functools.partial(layer_kernel, n, peers, chunks),
        out_shape=(
            out((narrow, nodes), BF16), out((narrow, nodes), BF16),
            out((2 * narrow, full), BF16),
        ),
        in_specs=[pl.BlockSpec(memory_space=vmem)] * 9,
        out_specs=[pl.BlockSpec(memory_space=vmem)] * 3,
        scratch_shapes=[
            vmem((nodes, nodes), BF16), vmem((nodes, every), BF16), vmem((nodes, every), BF16),
            vmem((peers * hubs, nodes), BF16), vmem((nodes, hubs), BF16), vmem((chunks, 16, width), F32),
            vmem((narrow, every), BF16), vmem((narrow, every), BF16),
            vmem((hubs, narrow), BF16), vmem((peers * hubs, narrow), BF16),
            vmem((full, 2 * narrow), BF16), vmem((chunks, n, narrow, width), F32),
            vmem((chunks, narrow, width), F32), vmem((chunks, 2 * narrow, width), BF16),
            vmem((chunks, n, narrow, width), BF16), vmem((chunks, n, narrow, width), BF16),
            vmem((chunks, n, narrow, width), BF16), vmem((chunks, n, narrow, width), BF16),
            vmem((chunks, n, narrow, width), BF16),
            vmem((chunks, narrow, width), F32), vmem((narrow, nodes), BF16),
            vmem((2 * narrow, full), F32), vmem((2 * narrow, full), BF16), vmem((peers // 2,) + piece, BF16),
            vmem((peers // 2,) + piece, BF16), vmem((peers // 2,) + piece, BF16),
            vmem(piece, BF16),
            vmem((narrow, every), BF16), vmem((narrow, every), BF16),
            vmem((peers * hubs, narrow), F32), vmem((peers, hubs, narrow), F32),
            pltpu.SemaphoreType.DMA((8, peers)), pltpu.SemaphoreType.DMA((8, peers)),
            pltpu.SemaphoreType.DMA((2, chunks, n)), pltpu.SemaphoreType.DMA((2, chunks, n)),
            pltpu.SemaphoreType.DMA((2, chunks, n)), pltpu.SemaphoreType.DMA((2, chunks, n)),
        ],
        compiler_params=pltpu.CompilerParams(
            collective_id=0, has_side_effects=True, vmem_limit_bytes=60 * 1024 * 1024
        ),
    )(
        feats, w_self, w_neigh, cotangent, loc_nbr.T, send_rows.reshape(1, -1),
        recv_node.reshape(1, -1), hub_rows.reshape(1, -1), hub_nbr.T,
    )
    grads = weight_all.astype(F32)
    return hidden, grad_feats, grads[:narrow], grads[narrow:]


def solution(mesh):
    return jax.shard_map(
        functools.partial(per_device, mesh.shape["col"], mesh.shape["row"]),
        mesh=mesh,
        in_specs=(
            P("col", "row"),
            P("col", None),
            P("col", None),
            P("col", "row"),
            P("row", None),
            P("row", None, None),
            P("row", None, None),
            P("row"),
            P("row", None),
        ),
        out_specs=(P("col", "row"), P("col", "row"), P("col", None), P("col", None)),
        check_vma=False,
    )
```
